512 devices in a mesh: tm: 16 (over x_hi, y, core), space: 32 (over z, x_lo).
Axes of the slice: x: 4 (x_hi: 2, x_lo: 2; x = x_hi * 2 + x_lo), y: 4, z: 16, core: 2. Of those that a mesh axis runs over, the one named last changes fastest.
Arguments:
- initial_states: float32 [16, 64, 32, 256], P('tm', 'space'), may hold values from -6 to 6
- velocity: float32 [3, 64, 32, 256], P(None, 'space'), may hold values from -2 to 2
- diffusivity: float32 [64, 32, 256], P('space'), may hold values from 0.005 to 0.05
Outputs:
- new_ends: float32 [16, 64, 32, 256], P('tm', 'space')
The draws below stay inside these ranges and needn't reach their ends.
All inputs are finite; a program needn't handle non-finite values.
Results may differ from the reference program's by a relative error of at most 0.00002.
Values sent between devices are 32-bit elements; how exact they have to be, the bound alone decides.
A program may use at most 64 MiB of HBM per device.

```python
import math
import jax
import jax.numpy as jnp
from jax import lax

CY = 32
CZ = 256
FINE_STEPS = 2
NT = 16
NX = 64


def block_scale(key, shape, split, smallest, largest):
    loudness, own = 1.0, jax.random.fold_in(key, 6)
    for position, blocks in split:
        steps = jnp.exp(jax.random.uniform(jax.random.fold_in(own, position), (blocks,), jnp.float32, smallest / len(split), largest / len(split)))
        loudness = loudness * jnp.repeat(steps, shape[position] // blocks).reshape([-1 if axis == position else 1 for axis in range(len(shape))])
    return loudness


def gaussian(stream_key, dims, scale, bound, shards=(), kind=jnp.bfloat16):
    entries = scale * jax.random.normal(stream_key, dims, jnp.float32)
    if shards:
        entries = entries * block_scale(stream_key, dims, shards, -0.22, 0.18)
    return jnp.clip(entries, -bound, bound).astype(kind)


def setup_inputs(seed: int = 0) -> dict:
    streams_of = jax.random.split(jax.random.key(seed), 4)
    initial_states = gaussian(streams_of[0], (NT, NX, CY, CZ), 1.0, 6.0, ((0, 16), (1, 32)), jnp.float32)
    velocity = gaussian(streams_of[1], (3, NX, CY, CZ), 0.15, 2.0, ((1, 32),), jnp.float32)
    diffusivity = jnp.clip(jnp.exp(math.log(0.05) - 2.3025851 * jax.random.uniform(streams_of[2], (NX, CY, CZ), jnp.float32) ** block_scale(streams_of[2], (NX, CY, CZ), ((0, 32),), -0.2, 0.2)), 0.005, 0.05)
    return {"initial_states": initial_states, "velocity": velocity, "diffusivity": diffusivity}


def restrict(field):
    leading = field.shape[:-3]
    shaped = field.reshape(leading + (field.shape[-3] // 2, 2, field.shape[-2] // 2, 2, field.shape[-1] // 2, 2))
    return jnp.mean(shaped, axis=(-5, -3, -1))


def prolong(field):
    return jnp.repeat(jnp.repeat(jnp.repeat(field, 2, axis=-3), 2, axis=-2), 2, axis=-1)


def advance(field, diffusivity, velocity, spread):
    padded = jnp.pad(field, 1)
    center = field
    x_plus = padded[2:, 1:-1, 1:-1]
    x_minus = padded[:-2, 1:-1, 1:-1]
    y_plus = padded[1:-1, 2:, 1:-1]
    y_minus = padded[1:-1, :-2, 1:-1]
    z_plus = padded[1:-1, 1:-1, 2:]
    z_minus = padded[1:-1, 1:-1, :-2]
    laplace = (x_plus + x_minus - 2.0 * center) + (y_plus + y_minus - 2.0 * center) + (z_plus + z_minus - 2.0 * center)
    drift_term = velocity[0] * (x_plus - x_minus) + velocity[1] * (y_plus - y_minus) + velocity[2] * (z_plus - z_minus)
    return center + spread * diffusivity * laplace - 0.5 * drift_term


def reference(initial_states, velocity, diffusivity):
    def fine_run(start):
        fine_field = start
        for section in range(FINE_STEPS):
            fine_field = advance(fine_field, diffusivity, velocity, 1.0)
        return fine_field

    fine_ends = jax.vmap(fine_run)(initial_states)
    coarse_diffusivity = restrict(diffusivity)
    coarse_velocity = restrict(velocity)

    def coarse(field):
        return advance(field, coarse_diffusivity, coarse_velocity, 0.5)

    coarse_start = restrict(initial_states)
    coarse_end = restrict(fine_ends)
    correction = coarse_end - jax.vmap(coarse)(coarse_start)

    def chain_step(carried, term):
        following = coarse(carried) + term
        return following, following

    unused, coarse_chain = lax.scan(chain_step, coarse_start[0], correction)
    return fine_ends + prolong(coarse_chain - coarse_end)
```

```python
import jax
import jax.numpy as jnp
from jax import lax
from jax.experimental import pallas as pl
from jax.experimental.pallas import tpu as pltpu
from jax.sharding import PartitionSpec as P

MESH = pl.DeviceIdType.MESH
REACH = 7
GREET = 8
NEAR = (1, 2, 3)
MID = 4
FAR = 8


def seven(diffusivity, vx, vy, vz, spread, first, last):
    ak = spread * diffusivity
    hx, hy, hz = 0.5 * vx, 0.5 * vy, 0.5 * vz
    rows = lax.broadcasted_iota(jnp.int32, ak.shape, ak.ndim - 2)
    cols = lax.broadcasted_iota(jnp.int32, ak.shape, ak.ndim - 1)
    zero = jnp.zeros_like(ak)
    return (
        1.0 - 6.0 * ak,
        (ak + hx) * first,
        (ak - hx) * last,
        jnp.where(rows == 0, zero, ak + hy),
        jnp.where(rows == ak.shape[-2] - 1, zero, ak - hy),
        jnp.where(cols == 0, zero, ak + hz),
        jnp.where(cols == ak.shape[-1] - 1, zero, ak - hz),
    )


def inplane(factors, f):
    c0, _, _, ym, yp, zm, zp = factors
    a, b = f.ndim - 2, f.ndim - 1
    return (
        c0 * f
        + (ym * pltpu.roll(f, 1, a) + yp * pltpu.roll(f, f.shape[a] - 1, a))
        + (zm * pltpu.roll(f, 1, b) + zp * pltpu.roll(f, f.shape[b] - 1, b))
    )


def restrict(work, two):
    rows = two.shape[1]
    both = two[0] + two[1]
    lanes = lax.broadcasted_iota(jnp.int32, (rows // 2, 128), 1)
    place = lax.rem(2 * lanes, 128)
    sides = []
    for h in range(2):
        work[h] = both[:, 128 * h : 128 * (h + 1)]
        half = work[h, pl.ds(0, rows // 2, 2), :] + work[h, pl.ds(1, rows // 2, 2), :]
        half = half + pltpu.roll(half, 127, 1)
        sides.append(jnp.take_along_axis(half, place, axis=1))
    return 0.125 * jnp.where(lanes < 64, sides[0], sides[1])


def kernel(
    nt, ns, init, vel, dif, fine_out, delta_out,
    f_ref, v_ref, k_ref, work, left0, right0, left1, right1, mid1,
    start_own, start_left, start_right, coef, kap,
    r_ref, u_ref, w_ref, near1, near2, near3, mid, far,
    load_sem, halo_send, halo_recv, coef_send, coef_recv, hop_send, hop_recv, ready,
):
    t, s = lax.axis_index("tm"), lax.axis_index("space")
    core = lax.rem(t, 2)
    sibling = t + 1 - 2 * core
    near = (near1, near2, near3)

    def at(ds):
        return lax.rem(s + (ds + ns), ns)

    for j, slot in zip(NEAR, near):

        @pl.when(t < j)
        def _():
            slot[...] = jnp.zeros_like(slot)

    barrier = pltpu.get_barrier_semaphore()
    for k in range(1, GREET + 1):
        for ds in (k, -k):
            pl.semaphore_signal(barrier, inc=1, device_id=(t, at(ds)), device_id_type=MESH)
    pl.semaphore_signal(barrier, inc=1, device_id=(sibling, s), device_id_type=MESH)
    for j in NEAR + (MID, FAR):

        @pl.when(t + j < nt)
        def _():
            pl.semaphore_signal(barrier, inc=1, device_id=(t + j, s), device_id_type=MESH)

    loads = [
        pltpu.make_async_copy(a, b, load_sem.at[i])
        for i, (a, b) in enumerate(((init.at[0], f_ref), (vel, v_ref), (dif, k_ref)))
    ]
    for copy in loads:
        copy.start()
    senders = sum(jnp.where(t >= j, 1, 0) for j in NEAR + (MID, FAR))
    pl.semaphore_wait(barrier, 2 * GREET + 1 + senders)

    def remote(src, dst, send, recv, tt, ds):
        return pltpu.make_async_remote_copy(
            src_ref=src, dst_ref=dst, send_sem=send, recv_sem=recv, device_id=(tt, at(ds)), device_id_type=MESH
        )

    halo0 = [
        remote(init.at[0, 0], right0, halo_send.at[0], halo_recv.at[0], t, -1),
        remote(init.at[0, 1], left0, halo_send.at[1], halo_recv.at[1], t, 1),
    ]
    for copy in halo0:
        copy.start()

    for i, j in enumerate(NEAR + (MID, FAR)):

        @pl.when(t >= j)
        def _():
            pl.semaphore_signal(ready.at[i], inc=1, device_id=(t - j, s), device_id_type=MESH)

    loads[0].wait()
    start = restrict(work, f_ref)
    start_own[...] = start
    halo_c = [
        remote(start_own, start_right, halo_send.at[2], halo_recv.at[2], t, -1),
        remote(start_own, start_left, halo_send.at[3], halo_recv.at[3], t, 1),
    ]
    for copy in halo_c:
        copy.start()

    loads[1].wait()
    loads[2].wait()
    coarse = [restrict(work, v_ref[0]), restrict(work, v_ref[1]), restrict(work, v_ref[2]), restrict(work, k_ref)]
    for i in range(2):
        coef[core, REACH, i] = jnp.where(core == 0, coarse[i], coarse[2 + i])
    coef_out = []
    for k in range(1, REACH + 1):
        for ds in (k, -k):
            copy = remote(coef.at[core, REACH], coef.at[core, REACH - ds], coef_send.at[0], coef_recv.at[0], t, ds)
            copy.start()
            coef_out.append(copy)

    one = jnp.float32(1.0)
    first = jnp.where(s == 0, 0.0, one)
    last = jnp.where(s == ns - 1, 0.0, one)
    fine0 = seven(k_ref[0], v_ref[0, 0], v_ref[1, 0], v_ref[2, 0], 1.0, first, one)
    fine1 = seven(k_ref[1], v_ref[0, 1], v_ref[1, 1], v_ref[2, 1], 1.0, one, last)

    def partial(a, b):
        return inplane(fine0, a) + fine0[2] * b, inplane(fine1, b) + fine1[1] * a

    pa, pb = partial(f_ref[0], f_ref[1])
    for copy in halo0:
        copy.wait_recv()
    mid1[0] = pa + fine0[1] * left0[...]
    mid1[1] = pb + fine1[2] * right0[...]
    halo1 = [
        remote(mid1.at[0], right1, halo_send.at[4], halo_recv.at[4], t, -1),
        remote(mid1.at[1], left1, halo_send.at[5], halo_recv.at[5], t, 1),
    ]
    for copy in halo1:
        copy.start()

    pa, pb = partial(mid1[0], mid1[1])
    own = seven(coarse[3], coarse[0], coarse[1], coarse[2], 0.5, first, last)
    for copy in halo_c:
        copy.wait_recv()
    stepped = inplane(own, start) + (own[1] * start_left[...] + own[2] * start_right[...])
    for copy in halo1:
        copy.wait_recv()
    fine_out[0] = pa + fine0[1] * left1[...]
    fine_out[1] = pb + fine1[2] * right1[...]
    end = restrict(work, fine_out)
    r_ref[...] = end - jnp.where(t == 0, 0.0, one) * stepped

    def hop(number, dt, src, slot):
        @pl.when(t + dt < nt)
        def _():
            pl.semaphore_wait(ready.at[number], 1)
            for ds in range(-dt, dt + 1):
                remote(src, slot.at[dt - ds], hop_send.at[number], hop_recv.at[number], t + dt, ds).start()

    def arrived(number, dt, slot):
        @pl.when(t >= dt)
        def _():
            pltpu.make_async_copy(slot, slot, hop_recv.at[number]).wait()

    def sent(number, dt, slot):
        @pl.when(t + dt < nt)
        def _():
            pltpu.make_async_copy(slot, slot, hop_send.at[number]).wait()

    for i, j in enumerate(NEAR):
        hop(i, j, r_ref, near[i])

    some = coef.at[0, 0 : 2 * REACH]
    pltpu.make_async_copy(some, some, coef_recv.at[0]).wait()
    share = remote(coef.at[core], coef.at[core], coef_send.at[1], coef_recv.at[1], sibling, 0)
    share.start()
    share.wait_recv()
    for p in range(-REACH, REACH + 1):
        i = p + REACH
        position = at(p)
        factors = seven(
            coef[1, i, 1], coef[0, i, 0], coef[0, i, 1], coef[1, i, 0], 0.5,
            jnp.where(position == 0, 0.0, one), jnp.where(position == ns - 1, 0.0, one),
        )
        for n in range(7):
            kap[n, i] = factors[n]

    def coarse_step(v):
        w = (v.shape[0] - 3) // 2
        factors = [kap[n, REACH - w : REACH + w + 1] for n in range(7)]
        return inplane(factors, v[1:-1]) + (factors[1] * v[:-2] + factors[2] * v[2:])

    for i, j in enumerate(NEAR):
        arrived(i, j, near[i])
    v = near3[...]
    v = coarse_step(v) + near2[...]
    v = coarse_step(v) + near1[...]
    u_ref[...] = coarse_step(v)[0] + r_ref[...]

    hop(3, MID, u_ref, mid)
    arrived(3, MID, mid)

    @pl.when(t >= MID)
    def _():
        v = mid[...]
        for _ in range(MID):
            v = coarse_step(v)
        w_ref[...] = v[0] + u_ref[...]

    @pl.when(t < MID)
    def _():
        w_ref[...] = u_ref[...]

    hop(4, FAR, w_ref, far)
    arrived(4, FAR, far)

    def finish(c):
        d = c - end
        lanes = lax.broadcasted_iota(jnp.int32, d.shape, 1)
        for h in range(2):
            wide = jnp.take_along_axis(d, lanes // 2 + 64 * h, axis=1)
            for i in range(2):
                work[h, pl.ds(i, d.shape[0], 2), :] = wide
            delta_out[:, 128 * h : 128 * (h + 1)] = work[h]

    @pl.when(t >= FAR)
    def _():
        v = far[...]
        for _ in range(FAR):
            v = coarse_step(v)
        finish(v[0] + w_ref[...])

    @pl.when(t < FAR)
    def _():
        finish(w_ref[...])

    for copy in halo0 + halo_c + halo1:
        copy.wait_send()
    pltpu.make_async_copy(some, some, coef_send.at[0]).wait()
    share.wait_send()
    for i, j in enumerate(NEAR):
        sent(i, j, near[i])
    sent(3, MID, mid)
    sent(4, FAR, far)


def solution(mesh):
    nt, ns = mesh.shape["tm"], mesh.shape["space"]

    def shards(initial_states, velocity, diffusivity):
        _, planes, cy, cz = initial_states.shape
        fine = (planes, cy, cz)
        plane, small = (cy, cz), (cy // 2, cz // 2)

        def vmem(*shape):
            return pltpu.VMEM(shape, jnp.float32)

        dma = pltpu.SemaphoreType.DMA
        ended, delta = pl.pallas_call(
            lambda *refs: kernel(nt, ns, *refs),
            out_shape=(jax.ShapeDtypeStruct(fine, jnp.float32), jax.ShapeDtypeStruct(plane, jnp.float32)),
            in_specs=[pl.BlockSpec(memory_space=pl.ANY)] * 3,
            out_specs=(pl.BlockSpec(memory_space=pltpu.VMEM),) * 2,
            scratch_shapes=[
                vmem(*fine), vmem(3, *fine), vmem(*fine), vmem(2, cy, cz // 2),
                vmem(*plane), vmem(*plane), vmem(*plane), vmem(*plane), vmem(*fine),
                vmem(*small), vmem(*small), vmem(*small),
                vmem(2, 2 * REACH + 1, 2, *small), vmem(7, 2 * REACH + 1, *small),
                vmem(*small), vmem(*small), vmem(*small),
                *(vmem(2 * j + 1, *small) for j in NEAR), vmem(2 * MID + 1, *small), vmem(2 * FAR + 1, *small),
                dma((3,)), dma((6,)), dma((6,)), dma((2,)), dma((2,)), dma((5,)), dma((5,)),
                pltpu.SemaphoreType.REGULAR((5,)),
            ],
            compiler_params=pltpu.CompilerParams(collective_id=0, has_side_effects=True),
        )(initial_states, velocity, diffusivity)
        return (ended + delta[None])[None]

    in_specs = (P("tm", "space", None, None), P(None, "space", None, None), P("space", None, None))
    out_specs = P("tm", "space", None, None)
    return jax.shard_map(shards, mesh=mesh, in_specs=in_specs, out_specs=out_specs, check_vma=False)
```

```python
import functools

import jax
import jax.numpy as jnp
from jax import lax
from jax.experimental import pallas as pl
from jax.experimental.pallas import tpu as pltpu
from jax.sharding import PartitionSpec as P

MESH = pl.DeviceIdType.MESH
REACH = 7
GREET = 8
NEAR = (1, 2, 3)
MID = 4
FAR = 8


def seven(diffusivity, vx, vy, vz, spread):
    ak = spread * diffusivity
    hx, hy, hz = 0.5 * vx, 0.5 * vy, 0.5 * vz
    rows = lax.broadcasted_iota(jnp.int32, ak.shape, ak.ndim - 2)
    cols = lax.broadcasted_iota(jnp.int32, ak.shape, ak.ndim - 1)
    zero = jnp.zeros_like(ak)
    return (
        1.0 - 6.0 * ak,
        ak + hx,
        ak - hx,
        jnp.where(rows == 0, zero, ak + hy),
        jnp.where(rows == ak.shape[-2] - 1, zero, ak - hy),
        jnp.where(cols == 0, zero, ak + hz),
        jnp.where(cols == ak.shape[-1] - 1, zero, ak - hz),
    )


def inplane(factors, f):
    c0, _, _, ym, yp, zm, zp = factors
    a, b = f.ndim - 2, f.ndim - 1
    return (
        c0 * f
        + (ym * pltpu.roll(f, 1, a) + yp * pltpu.roll(f, f.shape[a] - 1, a))
        + (zm * pltpu.roll(f, 1, b) + zp * pltpu.roll(f, f.shape[b] - 1, b))
    )


def restrict(work, two):
    rows = two.shape[1]
    both = two[0] + two[1]
    lanes = lax.broadcasted_iota(jnp.int32, (rows // 2, 128), 1)
    place = lax.rem(2 * lanes, 128)
    sides = []
    for h in range(2):
        work[h] = both[:, 128 * h : 128 * (h + 1)]
        half = work[h, pl.ds(0, rows // 2, 2), :] + work[h, pl.ds(1, rows // 2, 2), :]
        half = half + pltpu.roll(half, 127, 1)
        sides.append(jnp.take_along_axis(half, place, axis=1))
    return 0.125 * jnp.where(lanes < 64, sides[0], sides[1])


def kernel(
    nt, ns, init, vel, dif, fine_out, delta_out,
    f_ref, v_ref, k_ref, work, left0, right0, left1, right1, mid1,
    start_own, start_left, start_right, coef, kap,
    r_ref, u_ref, w_ref, near1, near2, near3, mid, far,
    load_sem, halo_send, halo_recv, coef_send, coef_recv, hop_send, hop_recv, ready,
):
    t, s = lax.axis_index("tm"), lax.axis_index("space")
    core = lax.rem(t, 2)
    sibling = t + 1 - 2 * core
    near = (near1, near2, near3)

    def inside(ds):
        return s + ds < ns if ds > 0 else s + ds >= 0

    def outward(width):
        return [ds for k in range(width, 0, -1) for ds in (k, -k)]

    for j, slot in zip(NEAR, near):

        @pl.when(t < j)
        def _():
            slot[...] = jnp.zeros_like(slot)

    @pl.when((s < FAR) | (s >= ns - FAR))
    def _():
        for slot in (near1, near2, near3, mid, far, coef):
            slot[...] = jnp.zeros_like(slot)

    @pl.when(s == 0)
    def _():
        for slot in (left0, left1, start_left):
            slot[...] = jnp.zeros_like(slot)

    @pl.when(s == ns - 1)
    def _():
        for slot in (right0, right1, start_right):
            slot[...] = jnp.zeros_like(slot)

    barrier = pltpu.get_barrier_semaphore()
    for ds in reversed(outward(GREET)):

        @pl.when(inside(ds))
        def _():
            pl.semaphore_signal(barrier, inc=1, device_id=(t, s + ds), device_id_type=MESH)

    pl.semaphore_signal(barrier, inc=1, device_id=(sibling, s), device_id_type=MESH)
    for j in NEAR + (MID, FAR):

        @pl.when(t + j < nt)
        def _():
            pl.semaphore_signal(barrier, inc=1, device_id=(t + j, s), device_id_type=MESH)

    loads = [
        pltpu.make_async_copy(a, b, load_sem.at[i])
        for i, (a, b) in enumerate(((init.at[0], f_ref), (vel, v_ref), (dif, k_ref)))
    ]
    for copy in loads:
        copy.start()
    senders = sum(jnp.where(t >= j, 1, 0) for j in NEAR + (MID, FAR))
    beside = jnp.minimum(s, GREET) + jnp.minimum(ns - 1 - s, GREET)
    pl.semaphore_wait(barrier, beside + 1 + senders)

    def remote(src, dst, send, recv, tt, ds):
        return pltpu.make_async_remote_copy(
            src_ref=src, dst_ref=dst, send_sem=send, recv_sem=recv, device_id=(tt, s + ds), device_id_type=MESH
        )

    def beside_do(pair, what):
        down, up = pair

        @pl.when(s > 0)
        def _():
            if what == "start":
                down.start()
            elif what == "recv":
                up.wait_recv()
            else:
                down.wait_send()

        @pl.when(s < ns - 1)
        def _():
            if what == "start":
                up.start()
            elif what == "recv":
                down.wait_recv()
            else:
                up.wait_send()

    loads[0].wait()
    halo0 = [
        remote(f_ref.at[0], right0, halo_send.at[0], halo_recv.at[0], t, -1),
        remote(f_ref.at[1], left0, halo_send.at[1], halo_recv.at[1], t, 1),
    ]
    beside_do(halo0, "start")

    for i, j in enumerate(NEAR + (MID, FAR)):

        @pl.when(t >= j)
        def _():
            pl.semaphore_signal(ready.at[i], inc=1, device_id=(t - j, s), device_id_type=MESH)

    start = restrict(work, f_ref)
    start_own[...] = start
    halo_c = [
        remote(start_own, start_right, halo_send.at[2], halo_recv.at[2], t, -1),
        remote(start_own, start_left, halo_send.at[3], halo_recv.at[3], t, 1),
    ]
    beside_do(halo_c, "start")

    loads[1].wait()
    loads[2].wait()
    coarse = [restrict(work, v_ref[0]), restrict(work, v_ref[1]), restrict(work, v_ref[2]), restrict(work, k_ref)]
    for i in range(2):
        coef[core, REACH, i] = jnp.where(core == 0, coarse[i], coarse[2 + i])
    for ds in reversed(outward(REACH)):

        @pl.when(inside(ds))
        def _():
            i = REACH - ds
            remote(coef.at[core, REACH], coef.at[core, i], coef_send.at[i], coef_recv.at[i], t, ds).start()


    one = jnp.float32(1.0)
    fine0 = seven(k_ref[0], v_ref[0, 0], v_ref[1, 0], v_ref[2, 0], 1.0)
    fine1 = seven(k_ref[1], v_ref[0, 1], v_ref[1, 1], v_ref[2, 1], 1.0)

    def partial(a, b):
        return inplane(fine0, a) + fine0[2] * b, inplane(fine1, b) + fine1[1] * a

    pa, pb = partial(f_ref[0], f_ref[1])
    beside_do(halo0, "recv")
    mid1[0] = pa + fine0[1] * left0[...]
    mid1[1] = pb + fine1[2] * right0[...]
    halo1 = [
        remote(mid1.at[0], right1, halo_send.at[4], halo_recv.at[4], t, -1),
        remote(mid1.at[1], left1, halo_send.at[5], halo_recv.at[5], t, 1),
    ]
    beside_do(halo1, "start")

    pa, pb = partial(mid1[0], mid1[1])
    own = seven(coarse[3], coarse[0], coarse[1], coarse[2], 0.5)
    beside_do(halo_c, "recv")
    stepped = inplane(own, start) + (own[1] * start_left[...] + own[2] * start_right[...])
    beside_do(halo1, "recv")
    fine_out[0] = pa + fine0[1] * left1[...]
    fine_out[1] = pb + fine1[2] * right1[...]
    end = restrict(work, fine_out)
    r_ref[...] = end - jnp.where(t == 0, 0.0, one) * stepped

    def each(width, slot, sem, mirrored):
        low, high = jnp.minimum(s, width), jnp.minimum(ns - 1 - s, width)
        if mirrored:
            low, high = high, low

        def one_of(i, _):
            pltpu.make_async_copy(slot(i), slot(i), sem(i)).wait()
            return 0

        lax.fori_loop(width - low, width + high + 1, one_of, 0)

    def hop(number, dt, src, slot):
        @pl.when(t + dt < nt)
        def _():
            pl.semaphore_wait(ready.at[number], 1)

            def send(ds):
                i = dt - ds
                remote(src, slot.at[i], hop_send.at[number, i], hop_recv.at[number, i], t + dt, ds).start()

            for ds in outward(dt):
                pl.when(inside(ds))(functools.partial(send, ds))
            send(0)

    def arrived(number, dt, slot):
        @pl.when(t >= dt)
        def _():
            each(dt, lambda i: slot.at[i], lambda i: hop_recv.at[number, i], False)

    def sent(number, dt, slot):
        @pl.when(t + dt < nt)
        def _():
            each(dt, lambda i: slot.at[i], lambda i: hop_send.at[number, i], True)

    for i, j in enumerate(NEAR):
        hop(i, j, r_ref, near[i])

    def around(sem, mirrored):
        low, high = jnp.minimum(s, REACH), jnp.minimum(ns - 1 - s, REACH)
        if mirrored:
            low, high = high, low

        def one_of(i, _):
            pltpu.make_async_copy(coef.at[core, i], coef.at[core, i], sem.at[i]).wait()
            return 0

        lax.fori_loop(REACH - low, REACH, one_of, 0)
        lax.fori_loop(REACH + 1, REACH + high + 1, one_of, 0)

    around(coef_recv, False)
    share = remote(coef.at[core], coef.at[core], coef_send.at[REACH], coef_recv.at[REACH], sibling, 0)
    share.start()
    share.wait_recv()
    for p in range(-REACH, REACH + 1):
        i = p + REACH
        factors = seven(coef[1, i, 1], coef[0, i, 0], coef[0, i, 1], coef[1, i, 0], 0.5)
        for n in range(7):
            kap[n, i] = factors[n]

    def coarse_step(v):
        w = (v.shape[0] - 3) // 2
        factors = [kap[n, REACH - w : REACH + w + 1] for n in range(7)]
        return inplane(factors, v[1:-1]) + (factors[1] * v[:-2] + factors[2] * v[2:])

    for i, j in enumerate(NEAR):
        arrived(i, j, near[i])
    v = near3[...]
    v = coarse_step(v) + near2[...]
    v = coarse_step(v) + near1[...]
    u_ref[...] = coarse_step(v)[0] + r_ref[...]

    hop(3, MID, u_ref, mid)
    arrived(3, MID, mid)

    @pl.when(t >= MID)
    def _():
        v = mid[...]
        for _ in range(MID):
            v = coarse_step(v)
        w_ref[...] = v[0] + u_ref[...]

    @pl.when(t < MID)
    def _():
        w_ref[...] = u_ref[...]

    hop(4, FAR, w_ref, far)
    arrived(4, FAR, far)

    def finish(c):
        d = c - end
        lanes = lax.broadcasted_iota(jnp.int32, d.shape, 1)
        for h in range(2):
            wide = jnp.take_along_axis(d, lanes // 2 + 64 * h, axis=1)
            for i in range(2):
                work[h, pl.ds(i, d.shape[0], 2), :] = wide
            delta_out[:, 128 * h : 128 * (h + 1)] = work[h]

    @pl.when(t >= FAR)
    def _():
        v = far[...]
        for _ in range(FAR):
            v = coarse_step(v)
        finish(v[0] + w_ref[...])

    @pl.when(t < FAR)
    def _():
        finish(w_ref[...])

    for pair in (halo0, halo_c, halo1):
        beside_do(pair, "send")
    around(coef_send, True)
    share.wait_send()
    for i, j in enumerate(NEAR):
        sent(i, j, near[i])
    sent(3, MID, mid)
    sent(4, FAR, far)


def solution(mesh):
    nt, ns = mesh.shape["tm"], mesh.shape["space"]

    def shards(initial_states, velocity, diffusivity):
        _, planes, cy, cz = initial_states.shape
        fine = (planes, cy, cz)
        plane, small = (cy, cz), (cy // 2, cz // 2)

        def vmem(*shape):
            return pltpu.VMEM(shape, jnp.float32)

        dma = pltpu.SemaphoreType.DMA
        ended, delta = pl.pallas_call(
            lambda *refs: kernel(nt, ns, *refs),
            out_shape=(jax.ShapeDtypeStruct(fine, jnp.float32), jax.ShapeDtypeStruct(plane, jnp.float32)),
            in_specs=[pl.BlockSpec(memory_space=pltpu.HBM)] * 3,
            out_specs=(pl.BlockSpec(memory_space=pltpu.VMEM),) * 2,
            scratch_shapes=[
                vmem(*fine), vmem(3, *fine), vmem(*fine), vmem(2, cy, cz // 2),
                vmem(*plane), vmem(*plane), vmem(*plane), vmem(*plane), vmem(*fine),
                vmem(*small), vmem(*small), vmem(*small),
                vmem(2, 2 * REACH + 1, 2, *small), vmem(7, 2 * REACH + 1, *small),
                vmem(*small), vmem(*small), vmem(*small),
                *(vmem(2 * j + 1, *small) for j in NEAR), vmem(2 * MID + 1, *small), vmem(2 * FAR + 1, *small),
                dma((3,)), dma((6,)), dma((6,)), dma((2 * REACH + 1,)), dma((2 * REACH + 1,)),
                dma((5, 2 * FAR + 1)), dma((5, 2 * FAR + 1)),
                pltpu.SemaphoreType.REGULAR((5,)),
            ],
            compiler_params=pltpu.CompilerParams(collective_id=0, has_side_effects=True, vmem_limit_bytes=56475648),
        )(initial_states, velocity, diffusivity)
        return (ended + delta[None])[None]

    in_specs = (P("tm", "space", None, None), P(None, "space", None, None), P("space", None, None))
    out_specs = P("tm", "space", None, None)
    return jax.shard_map(shards, mesh=mesh, in_specs=in_specs, out_specs=out_specs, check_vma=False)
```

```python
import functools

import jax
import jax.numpy as jnp
from jax import lax
from jax.experimental import pallas as pl
from jax.experimental.pallas import tpu as pltpu
from jax.sharding import PartitionSpec as P

MESH = pl.DeviceIdType.MESH
REACH = 7
INNER = 3
GREET = 8
NEAR = (1, 2, 3)
MID = 4
FAR = 8


def seven(diffusivity, vx, vy, vz, spread):
    ak = spread * diffusivity
    hx, hy, hz = 0.5 * vx, 0.5 * vy, 0.5 * vz
    rows = lax.broadcasted_iota(jnp.int32, ak.shape, ak.ndim - 2)
    cols = lax.broadcasted_iota(jnp.int32, ak.shape, ak.ndim - 1)
    zero = jnp.zeros_like(ak)
    return (
        1.0 - 6.0 * ak,
        ak + hx,
        ak - hx,
        jnp.where(rows == 0, zero, ak + hy),
        jnp.where(rows == ak.shape[-2] - 1, zero, ak - hy),
        jnp.where(cols == 0, zero, ak + hz),
        jnp.where(cols == ak.shape[-1] - 1, zero, ak - hz),
    )


def inplane(factors, f):
    c0, _, _, ym, yp, zm, zp = factors
    a, b = f.ndim - 2, f.ndim - 1
    return (
        c0 * f
        + (ym * pltpu.roll(f, 1, a) + yp * pltpu.roll(f, f.shape[a] - 1, a))
        + (zm * pltpu.roll(f, 1, b) + zp * pltpu.roll(f, f.shape[b] - 1, b))
    )


def restrict(work, two):
    rows = two.shape[1]
    both = two[0] + two[1]
    lanes = lax.broadcasted_iota(jnp.int32, (rows // 2, 128), 1)
    place = lax.rem(2 * lanes, 128)
    sides = []
    for h in range(2):
        work[h] = both[:, 128 * h : 128 * (h + 1)]
        half = work[h, pl.ds(0, rows // 2, 2), :] + work[h, pl.ds(1, rows // 2, 2), :]
        half = half + pltpu.roll(half, 127, 1)
        sides.append(jnp.take_along_axis(half, place, axis=1))
    return 0.125 * jnp.where(lanes < 64, sides[0], sides[1])


def kernel(
    nt, ns, init, vel, dif, fine_out, delta_out,
    f_ref, v_ref, k_ref, work, left0, right0, left1, right1, out_low, out_high,
    start_own, start_left, start_right, coef, kap,
    r_ref, u_ref, w_ref, near1, near2, near3, mid, far,
    load_sem, halo_send, halo_recv, coef_send, coef_recv, share_send, share_recv, hop_send, hop_recv, ready,
):
    t, s = lax.axis_index("tm"), lax.axis_index("space")
    core = lax.rem(t, 2)
    sibling = t + 1 - 2 * core
    near = (near1, near2, near3)

    def inside(ds):
        return s + ds < ns if ds > 0 else s + ds >= 0

    def outward(width):
        return [ds for k in range(width, 0, -1) for ds in (k, -k)]

    for j, slot in zip(NEAR, near):

        @pl.when(t < j)
        def _():
            slot[...] = jnp.zeros_like(slot)

    @pl.when((s < FAR) | (s >= ns - FAR))
    def _():
        for slot in (near1, near2, near3, mid, far, coef):
            slot[...] = jnp.zeros_like(slot)

    @pl.when(s == 0)
    def _():
        for slot in (left0, left1, start_left):
            slot[...] = jnp.zeros_like(slot)

    @pl.when(s == ns - 1)
    def _():
        for slot in (right0, right1, start_right):
            slot[...] = jnp.zeros_like(slot)

    barrier = pltpu.get_barrier_semaphore()
    for ds in reversed(outward(GREET)):

        @pl.when(inside(ds))
        def _():
            pl.semaphore_signal(barrier, inc=1, device_id=(t, s + ds), device_id_type=MESH)

    pl.semaphore_signal(barrier, inc=1, device_id=(sibling, s), device_id_type=MESH)
    for j in NEAR + (MID, FAR):

        @pl.when(t + j < nt)
        def _():
            pl.semaphore_signal(barrier, inc=1, device_id=(t + j, s), device_id_type=MESH)

    loads = [
        pltpu.make_async_copy(a, b, load_sem.at[i])
        for i, (a, b) in enumerate(((init.at[0], f_ref), (vel, v_ref), (dif, k_ref)))
    ]
    for copy in loads:
        copy.start()
    for copy in loads:
        copy.wait()
    fine0 = seven(k_ref[0], v_ref[0, 0], v_ref[1, 0], v_ref[2, 0], 1.0)
    fine1 = seven(k_ref[1], v_ref[0, 1], v_ref[1, 1], v_ref[2, 1], 1.0)

    def partial(a, b):
        return inplane(fine0, a) + fine0[2] * b, inplane(fine1, b) + fine1[1] * a

    pa, pb = partial(f_ref[0], f_ref[1])
    out_low[0], out_low[1] = fine0[1], pa
    out_high[0], out_high[1] = fine1[2], pb

    senders = sum(jnp.where(t >= j, 1, 0) for j in NEAR + (MID, FAR))
    beside = jnp.minimum(s, GREET) + jnp.minimum(ns - 1 - s, GREET)
    pl.semaphore_wait(barrier, beside + 1 + senders)

    def remote(src, dst, send, recv, tt, ds):
        return pltpu.make_async_remote_copy(
            src_ref=src, dst_ref=dst, send_sem=send, recv_sem=recv, device_id=(tt, s + ds), device_id_type=MESH
        )

    def beside_do(pair, what):
        down, up = pair

        @pl.when(s > 0)
        def _():
            if what == "start":
                down.start()
            elif what == "recv":
                up.wait_recv()
            else:
                down.wait_send()

        @pl.when(s < ns - 1)
        def _():
            if what == "start":
                up.start()
            elif what == "recv":
                down.wait_recv()
            else:
                up.wait_send()

    halo0 = [
        remote(f_ref.at[0], right0, halo_send.at[0], halo_recv.at[0], t, -1),
        remote(f_ref.at[1], left0, halo_send.at[1], halo_recv.at[1], t, 1),
    ]
    halo1 = [
        remote(out_low, right1, halo_send.at[4], halo_recv.at[4], t, -1),
        remote(out_high, left1, halo_send.at[5], halo_recv.at[5], t, 1),
    ]
    beside_do(halo0, "start")
    beside_do(halo1, "start")

    for i, j in enumerate(NEAR + (MID, FAR)):

        @pl.when(t >= j)
        def _():
            pl.semaphore_signal(ready.at[i], inc=1, device_id=(t - j, s), device_id_type=MESH)

    start = restrict(work, f_ref)
    start_own[...] = start
    halo_c = [
        remote(start_own, start_right, halo_send.at[2], halo_recv.at[2], t, -1),
        remote(start_own, start_left, halo_send.at[3], halo_recv.at[3], t, 1),
    ]
    beside_do(halo_c, "start")

    coarse = [restrict(work, v_ref[0]), restrict(work, v_ref[1]), restrict(work, v_ref[2]), restrict(work, k_ref)]
    for i in range(2):
        coef[core, REACH, i] = jnp.where(core == 0, coarse[i], coarse[2 + i])
    def spread(offsets):
        for ds in offsets:

            @pl.when(inside(ds))
            def _():
                i = REACH - ds
                remote(coef.at[core, REACH], coef.at[core, i], coef_send.at[i], coef_recv.at[i], t, ds).start()

    spread(reversed(outward(INNER)))

    one = jnp.float32(1.0)
    own = seven(coarse[3], coarse[0], coarse[1], coarse[2], 0.5)
    beside_do(halo_c, "recv")
    stepped = inplane(own, start) + (own[1] * start_left[...] + own[2] * start_right[...])
    beside_do(halo0, "recv")
    a = pa + fine0[1] * left0[...]
    b = pb + fine1[2] * right0[...]
    pa, pb = partial(a, b)
    beside_do(halo1, "recv")
    fine_out[0] = pa + fine0[1] * (left1[1] + left1[0] * f_ref[0])
    fine_out[1] = pb + fine1[2] * (right1[1] + right1[0] * f_ref[1])
    end = restrict(work, fine_out)
    r_ref[...] = end - jnp.where(t == 0, 0.0, one) * stepped

    def each(width, slot, sem, mirrored):
        low, high = jnp.minimum(s, width), jnp.minimum(ns - 1 - s, width)
        if mirrored:
            low, high = high, low

        def one_of(i, _):
            pltpu.make_async_copy(slot(i), slot(i), sem(i)).wait()
            return 0

        lax.fori_loop(width - low, width + high + 1, one_of, 0)

    def hop(number, dt, src, slot):
        @pl.when(t + dt < nt)
        def _():
            pl.semaphore_wait(ready.at[number], 1)

            def send(ds):
                i = dt - ds
                remote(src, slot.at[i], hop_send.at[number, i], hop_recv.at[number, i], t + dt, ds).start()

            for ds in outward(dt):
                pl.when(inside(ds))(functools.partial(send, ds))
            send(0)

    def arrived(number, dt, slot):
        @pl.when(t >= dt)
        def _():
            each(dt, lambda i: slot.at[i], lambda i: hop_recv.at[number, i], False)

    def sent(number, dt, slot):
        @pl.when(t + dt < nt)
        def _():
            each(dt, lambda i: slot.at[i], lambda i: hop_send.at[number, i], True)

    for i, j in enumerate(NEAR):
        hop(i, j, r_ref, near[i])

    def around(sem, mirrored, first, last):
        low, high = jnp.minimum(s, last), jnp.minimum(ns - 1 - s, last)
        if mirrored:
            low, high = high, low

        def one_of(i, _):
            pltpu.make_async_copy(coef.at[core, i], coef.at[core, i], sem.at[i]).wait()
            return 0

        lax.fori_loop(REACH - low, REACH - first + 1, one_of, 0)
        lax.fori_loop(REACH + first, REACH + high + 1, one_of, 0)

    def share(number, first, last):
        planes = coef.at[core, first:last]
        return remote(planes, planes, share_send.at[number], share_recv.at[number], sibling, 0)

    def factors_of(first, last):
        for i in range(first, last):
            factors = seven(coef[1, i, 1], coef[0, i, 0], coef[0, i, 1], coef[1, i, 0], 0.5)
            for n in range(7):
                kap[n, i] = factors[n]

    low, high = REACH - INNER, REACH + INNER + 1
    around(coef_recv, False, 1, INNER)
    inner = share(0, low, high)
    inner.start()
    outer = [share(1, 0, low), share(2, high, 2 * REACH + 1)]

    @pl.when(t >= FAR)
    def _():
        spread(reversed(outward(REACH)[: 2 * (REACH - INNER)]))

    inner.wait_recv()
    factors_of(low, high)

    def coarse_step(v):
        w = (v.shape[0] - 3) // 2
        factors = [kap[n, REACH - w : REACH + w + 1] for n in range(7)]
        return inplane(factors, v[1:-1]) + (factors[1] * v[:-2] + factors[2] * v[2:])

    for i, j in enumerate(NEAR):
        arrived(i, j, near[i])
    v = near3[...]
    v = coarse_step(v) + near2[...]
    v = coarse_step(v) + near1[...]
    u_ref[...] = coarse_step(v)[0] + r_ref[...]

    hop(3, MID, u_ref, mid)
    arrived(3, MID, mid)

    @pl.when(t >= MID)
    def _():
        v = mid[...]
        for _ in range(MID):
            v = coarse_step(v)
        w_ref[...] = v[0] + u_ref[...]

    @pl.when(t < MID)
    def _():
        w_ref[...] = u_ref[...]

    hop(4, FAR, w_ref, far)

    @pl.when(t >= FAR)
    def _():
        around(coef_recv, False, INNER + 1, REACH)
        for copy in outer:
            copy.start()
        for copy in outer:
            copy.wait_recv()
        factors_of(0, low)
        factors_of(high, 2 * REACH + 1)

    arrived(4, FAR, far)

    def finish(c):
        d = c - end
        lanes = lax.broadcasted_iota(jnp.int32, d.shape, 1)
        for h in range(2):
            wide = jnp.take_along_axis(d, lanes // 2 + 64 * h, axis=1)
            for i in range(2):
                work[h, pl.ds(i, d.shape[0], 2), :] = wide
            delta_out[:, 128 * h : 128 * (h + 1)] = work[h]

    @pl.when(t >= FAR)
    def _():
        v = far[...]
        for _ in range(FAR):
            v = coarse_step(v)
        finish(v[0] + w_ref[...])

    @pl.when(t < FAR)
    def _():
        finish(w_ref[...])

    for pair in (halo0, halo_c, halo1):
        beside_do(pair, "send")
    around(coef_send, True, 1, INNER)
    inner.wait_send()

    @pl.when(t >= FAR)
    def _():
        around(coef_send, True, INNER + 1, REACH)
        for copy in outer:
            copy.wait_send()

    for i, j in enumerate(NEAR):
        sent(i, j, near[i])
    sent(3, MID, mid)
    sent(4, FAR, far)


def solution(mesh):
    nt, ns = mesh.shape["tm"], mesh.shape["space"]

    def shards(initial_states, velocity, diffusivity):
        _, planes, cy, cz = initial_states.shape
        fine = (planes, cy, cz)
        plane, small = (cy, cz), (cy // 2, cz // 2)

        def vmem(*shape):
            return pltpu.VMEM(shape, jnp.float32)

        dma = pltpu.SemaphoreType.DMA
        ended, delta = pl.pallas_call(
            lambda *refs: kernel(nt, ns, *refs),
            out_shape=(jax.ShapeDtypeStruct(fine, jnp.float32), jax.ShapeDtypeStruct(plane, jnp.float32)),
            in_specs=[pl.BlockSpec(memory_space=pltpu.HBM)] * 3,
            out_specs=(pl.BlockSpec(memory_space=pltpu.VMEM),) * 2,
            scratch_shapes=[
                vmem(*fine), vmem(3, *fine), vmem(*fine), vmem(2, cy, cz // 2),
                vmem(*plane), vmem(*plane), vmem(*fine), vmem(*fine), vmem(*fine), vmem(*fine),
                vmem(*small), vmem(*small), vmem(*small),
                vmem(2, 2 * REACH + 1, 2, *small), vmem(7, 2 * REACH + 1, *small),
                vmem(*small), vmem(*small), vmem(*small),
                *(vmem(2 * j + 1, *small) for j in NEAR), vmem(2 * MID + 1, *small), vmem(2 * FAR + 1, *small),
                dma((3,)), dma((6,)), dma((6,)), dma((2 * REACH + 1,)), dma((2 * REACH + 1,)), dma((3,)), dma((3,)),
                dma((5, 2 * FAR + 1)), dma((5, 2 * FAR + 1)),
                pltpu.SemaphoreType.REGULAR((5,)),
            ],
            compiler_params=pltpu.CompilerParams(collective_id=0, has_side_effects=True, vmem_limit_bytes=56430000),
        )(initial_states, velocity, diffusivity)
        return (ended + delta[None])[None]

    in_specs = (P("tm", "space", None, None), P(None, "space", None, None), P("space", None, None))
    out_specs = P("tm", "space", None, None)
    return jax.shard_map(shards, mesh=mesh, in_specs=in_specs, out_specs=out_specs, check_vma=False)
```

```python
import functools

import jax
import jax.numpy as jnp
from jax import lax
from jax.experimental import pallas as pl
from jax.experimental.pallas import tpu as pltpu
from jax.sharding import PartitionSpec as P

MESH = pl.DeviceIdType.MESH
REACH = 7
INNER = 3
GREET = 4
NEAR = (1, 2, 3)
MID = 4
FAR = 8
HOPS = NEAR + (MID, FAR)


def seven(diffusivity, vx, vy, vz, spread):
    ak = spread * diffusivity
    hx, hy, hz = 0.5 * vx, 0.5 * vy, 0.5 * vz
    rows = lax.broadcasted_iota(jnp.int32, ak.shape, ak.ndim - 2)
    cols = lax.broadcasted_iota(jnp.int32, ak.shape, ak.ndim - 1)
    zero = jnp.zeros_like(ak)
    return (
        1.0 - 6.0 * ak,
        ak + hx,
        ak - hx,
        jnp.where(rows == 0, zero, ak + hy),
        jnp.where(rows == ak.shape[-2] - 1, zero, ak - hy),
        jnp.where(cols == 0, zero, ak + hz),
        jnp.where(cols == ak.shape[-1] - 1, zero, ak - hz),
    )


def inplane(factors, f):
    c0, _, _, ym, yp, zm, zp = factors
    a, b = f.ndim - 2, f.ndim - 1
    return (
        c0 * f
        + (ym * pltpu.roll(f, 1, a) + yp * pltpu.roll(f, f.shape[a] - 1, a))
        + (zm * pltpu.roll(f, 1, b) + zp * pltpu.roll(f, f.shape[b] - 1, b))
    )


def restrict(work, two):
    rows = two.shape[1]
    both = two[0] + two[1]
    lanes = lax.broadcasted_iota(jnp.int32, (rows // 2, 128), 1)
    place = lax.rem(2 * lanes, 128)
    sides = []
    for h in range(2):
        work[h] = both[:, 128 * h : 128 * (h + 1)]
        half = work[h, pl.ds(0, rows // 2, 2), :] + work[h, pl.ds(1, rows // 2, 2), :]
        half = half + pltpu.roll(half, 127, 1)
        sides.append(jnp.take_along_axis(half, place, axis=1))
    return 0.125 * jnp.where(lanes < 64, sides[0], sides[1])


def kernel(
    nt, ns, init, vel, dif, fine_out, delta_out,
    f_ref, v_ref, k_ref, work, left0, right0, left1, right1, out_low, out_high,
    start_own, start_left, start_right, coef, kap,
    r_ref, u_ref, w_ref, near1, near2, near3, mid, far,
    load_sem, halo_send, halo_recv, coef_send, coef_recv, share_send, hop_send, hop_recv, ready,
):
    t, s = lax.axis_index("tm"), lax.axis_index("space")
    seat = lax.rem(t, FAR)
    group = t - seat
    near = (near1, near2, near3)

    def inside(ds):
        return s + ds < ns if ds > 0 else s + ds >= 0

    def outward(width):
        return [ds for k in range(width, 0, -1) for ds in (k, -k)]

    for j, slot in zip(NEAR, near):

        @pl.when(t < j)
        def _():
            slot[...] = jnp.zeros_like(slot)

    @pl.when((s < FAR) | (s >= ns - FAR))
    def _():
        for slot in (near1, near2, near3, mid, far, coef):
            slot[...] = jnp.zeros_like(slot)

    @pl.when(s == 0)
    def _():
        for slot in (left0, left1, start_left):
            slot[...] = jnp.zeros_like(slot)

    @pl.when(s == ns - 1)
    def _():
        for slot in (right0, right1, start_right):
            slot[...] = jnp.zeros_like(slot)

    barrier = pltpu.get_barrier_semaphore()
    for ds in reversed(outward(GREET)):

        @pl.when(inside(ds))
        def _():
            pl.semaphore_signal(barrier, inc=1, device_id=(t, s + ds), device_id_type=MESH)

    for j in range(1, FAR + 1):

        @pl.when((t + j < nt) if j in HOPS else (seat + j < FAR))
        def _():
            pl.semaphore_signal(barrier, inc=1, device_id=(t + j, s), device_id_type=MESH)

    loads = [
        pltpu.make_async_copy(a, b, load_sem.at[i])
        for i, (a, b) in enumerate(((init.at[0], f_ref), (vel, v_ref), (dif, k_ref)))
    ]
    for copy in loads:
        copy.start()
    for copy in loads:
        copy.wait()
    fine0 = seven(k_ref[0], v_ref[0, 0], v_ref[1, 0], v_ref[2, 0], 1.0)
    fine1 = seven(k_ref[1], v_ref[0, 1], v_ref[1, 1], v_ref[2, 1], 1.0)

    def partial(a, b):
        return inplane(fine0, a) + fine0[2] * b, inplane(fine1, b) + fine1[1] * a

    pa, pb = partial(f_ref[0], f_ref[1])
    out_low[0], out_low[1] = fine0[1], pa
    out_high[0], out_high[1] = fine1[2], pb

    start = restrict(work.at[0], f_ref)
    start_own[...] = start
    coarse = [restrict(work.at[1 + i], v_ref[i]) for i in range(3)]
    coarse.append(restrict(work.at[4], k_ref))
    for i in range(4):
        coef[REACH, i] = coarse[i]

    senders = sum(jnp.where((t if j in HOPS else seat) >= j, 1, 0) for j in range(1, FAR + 1))
    beside = jnp.minimum(s, GREET) + jnp.minimum(ns - 1 - s, GREET)
    pl.semaphore_wait(barrier, beside + senders)

    def remote(src, dst, send, recv, tt, ds):
        return pltpu.make_async_remote_copy(
            src_ref=src, dst_ref=dst, send_sem=send, recv_sem=recv, device_id=(tt, s + ds), device_id_type=MESH
        )

    def beside_do(pair, what):
        down, up = pair

        @pl.when(s > 0)
        def _():
            if what == "start":
                down.start()
            elif what == "recv":
                up.wait_recv()
            else:
                down.wait_send()

        @pl.when(s < ns - 1)
        def _():
            if what == "start":
                up.start()
            elif what == "recv":
                down.wait_recv()
            else:
                up.wait_send()

    halo0 = [
        remote(f_ref.at[0], right0, halo_send.at[0], halo_recv.at[0], t, -1),
        remote(f_ref.at[1], left0, halo_send.at[1], halo_recv.at[1], t, 1),
    ]
    halo1 = [
        remote(out_low, right1, halo_send.at[4], halo_recv.at[4], t, -1),
        remote(out_high, left1, halo_send.at[5], halo_recv.at[5], t, 1),
    ]
    halo_c = [
        remote(start_own, start_right, halo_send.at[2], halo_recv.at[2], t, -1),
        remote(start_own, start_left, halo_send.at[3], halo_recv.at[3], t, 1),
    ]
    def reach(off):
        return (s + off >= 0) & (s + off < ns)

    inner = (seat < 2 * INNER, jnp.where(seat < INNER, seat - INNER, seat - INNER + 1))
    outer = (group > 0, jnp.where(seat < REACH - INNER, seat - REACH, seat))

    def fetch(who, i):
        needed, off = who

        @pl.when(needed & reach(-off))
        def _():
            there = REACH + off
            remote(coef.at[REACH], coef.at[there], coef_send.at[i], coef_recv.at[there], t, -off).start()

    def fetched(who, i):
        needed, off = who

        @pl.when(needed & reach(-off))
        def _():
            pltpu.make_async_copy(coef.at[REACH], coef.at[REACH], coef_send.at[i]).wait()

    def hand_on(who, i):
        needed, off = who

        @pl.when(needed & reach(off))
        def _():
            here = REACH + off
            pltpu.make_async_copy(coef.at[here], coef.at[here], coef_recv.at[here]).wait()
            for turn in (4, 3, 5, 2, 6, 1, 7):
                to = group + lax.rem(seat + turn, FAR)
                remote(coef.at[here], coef.at[here], share_send.at[i, turn], coef_recv.at[here], to, 0).start()

    def handed_on(who, i):
        needed, off = who

        @pl.when(needed & reach(off))
        def _():
            for turn in range(1, FAR):
                pltpu.make_async_copy(coef.at[REACH], coef.at[REACH], share_send.at[i, turn]).wait()

    def handed(who, offs):
        needed, off = who
        for o in offs:

            @pl.when(inside(o) & (jnp.logical_not(needed) | (off != o)))
            def _():
                pltpu.make_async_copy(coef.at[REACH + o], coef.at[REACH + o], coef_recv.at[REACH + o]).wait()

    beside_do(halo0, "start")
    fetch(inner, 0)
    beside_do(halo1, "start")
    beside_do(halo_c, "start")
    for i, j in enumerate(HOPS[:-1]):

        @pl.when(t >= j)
        def _():
            pl.semaphore_signal(ready.at[i], inc=1, device_id=(t - j, s), device_id_type=MESH)

    for j in range(1, FAR):

        @pl.when(seat >= j)
        def _():
            pl.semaphore_signal(ready.at[5], inc=1, device_id=(t - j, s), device_id_type=MESH)

    @pl.when(seat < FAR - 1)
    def _():
        pl.semaphore_wait(ready.at[5], FAR - 1 - seat)

    @pl.when(group > 0)
    def _():
        for ds in (GREET, -GREET):

            @pl.when(inside(ds))
            def _():
                pl.semaphore_signal(ready.at[6], inc=1, device_id=(t, s + ds), device_id_type=MESH)

    hand_on(inner, 0)

    one = jnp.float32(1.0)
    own = seven(coarse[3], coarse[0], coarse[1], coarse[2], 0.5)
    beside_do(halo_c, "recv")
    stepped = inplane(own, start) + (own[1] * start_left[...] + own[2] * start_right[...])
    beside_do(halo0, "recv")
    a = pa + fine0[1] * left0[...]
    b = pb + fine1[2] * right0[...]
    pa, pb = partial(a, b)
    beside_do(halo1, "recv")
    fine_out[0] = pa + fine0[1] * (left1[1] + left1[0] * f_ref[0])
    fine_out[1] = pb + fine1[2] * (right1[1] + right1[0] * f_ref[1])
    end = restrict(work.at[0], fine_out)
    r_ref[...] = end - jnp.where(t == 0, 0.0, one) * stepped

    def each(width, slot, sem, mirrored):
        low, high = jnp.minimum(s, width), jnp.minimum(ns - 1 - s, width)
        if mirrored:
            low, high = high, low

        def one_of(i, _):
            pltpu.make_async_copy(slot(i), slot(i), sem(i)).wait()
            return 0

        lax.fori_loop(width - low, width + high + 1, one_of, 0)

    def hop(number, dt, src, slot):
        @pl.when(t + dt < nt)
        def _():
            pl.semaphore_wait(ready.at[number], 1)

            def send(ds):
                i = dt - ds
                remote(src, slot.at[i], hop_send.at[number, i], hop_recv.at[number, i], t + dt, ds).start()

            for ds in outward(dt):
                pl.when(inside(ds))(functools.partial(send, ds))
            send(0)

    def arrived(number, dt, slot):
        @pl.when(t >= dt)
        def _():
            each(dt, lambda i: slot.at[i], lambda i: hop_recv.at[number, i], False)

    def sent(number, dt, slot):
        @pl.when(t + dt < nt)
        def _():
            each(dt, lambda i: slot.at[i], lambda i: hop_send.at[number, i], True)

    for i, j in enumerate(NEAR):
        hop(i, j, r_ref, near[i])

    def factors_of(first, last):
        for i in range(first, last):
            factors = seven(coef[i, 3], coef[i, 0], coef[i, 1], coef[i, 2], 0.5)
            for n in range(7):
                kap[n, i] = factors[n]

    low, high = REACH - INNER, REACH + INNER + 1
    @pl.when(group > 0)
    def _():
        pl.semaphore_wait(ready.at[6], jnp.where(inside(GREET), 1, 0) + jnp.where(inside(-GREET), 1, 0))
        pl.semaphore_signal(ready.at[len(HOPS) - 1], inc=1, device_id=(t - FAR, s), device_id_type=MESH)

    fetch(outer, 1)
    handed(inner, [o for o in range(-INNER, INNER + 1) if o])
    factors_of(low, high)

    def coarse_step(v):
        w = (v.shape[0] - 3) // 2
        factors = [kap[n, REACH - w : REACH + w + 1] for n in range(7)]
        return inplane(factors, v[1:-1]) + (factors[1] * v[:-2] + factors[2] * v[2:])

    for i, j in enumerate(NEAR):
        arrived(i, j, near[i])
    v = near3[...]
    v = coarse_step(v) + near2[...]
    v = coarse_step(v) + near1[...]
    u_ref[...] = coarse_step(v)[0] + r_ref[...]

    hop(3, MID, u_ref, mid)
    hand_on(outer, 1)
    arrived(3, MID, mid)

    @pl.when(t >= MID)
    def _():
        v = mid[...]
        for _ in range(MID):
            v = coarse_step(v)
        w_ref[...] = v[0] + u_ref[...]

    @pl.when(t < MID)
    def _():
        w_ref[...] = u_ref[...]

    hop(4, FAR, w_ref, far)

    for pair in (halo0, halo_c, halo1):
        beside_do(pair, "send")
    fetched(inner, 0)
    fetched(outer, 1)
    handed_on(inner, 0)
    handed_on(outer, 1)
    for i, j in enumerate(NEAR):
        sent(i, j, near[i])
    sent(3, MID, mid)

    @pl.when(t >= FAR)
    def _():
        handed(outer, [o for o in range(-REACH, REACH + 1) if abs(o) > INNER])
        factors_of(0, low)
        factors_of(high, 2 * REACH + 1)

    arrived(4, FAR, far)

    def finish(c):
        d = c - end
        lanes = lax.broadcasted_iota(jnp.int32, d.shape, 1)
        for h in range(2):
            wide = jnp.take_along_axis(d, lanes // 2 + 64 * h, axis=1)
            for i in range(2):
                work[0, h, pl.ds(i, d.shape[0], 2), :] = wide
            delta_out[:, 128 * h : 128 * (h + 1)] = work[0, h]

    @pl.when(t >= FAR)
    def _():
        v = far[...]
        for _ in range(FAR):
            v = coarse_step(v)
        finish(v[0] + w_ref[...])

    @pl.when(t < FAR)
    def _():
        finish(w_ref[...])

    sent(4, FAR, far)


def solution(mesh):
    nt, ns = mesh.shape["tm"], mesh.shape["space"]

    def shards(initial_states, velocity, diffusivity):
        _, planes, cy, cz = initial_states.shape
        fine = (planes, cy, cz)
        plane, small = (cy, cz), (cy // 2, cz // 2)

        def vmem(*shape):
            return pltpu.VMEM(shape, jnp.float32)

        dma = pltpu.SemaphoreType.DMA
        ended, delta = pl.pallas_call(
            lambda *refs: kernel(nt, ns, *refs),
            out_shape=(jax.ShapeDtypeStruct(fine, jnp.float32), jax.ShapeDtypeStruct(plane, jnp.float32)),
            in_specs=[pl.BlockSpec(memory_space=pltpu.HBM)] * 3,
            out_specs=(pl.BlockSpec(memory_space=pltpu.VMEM),) * 2,
            scratch_shapes=[
                vmem(*fine), vmem(3, *fine), vmem(*fine), vmem(5, 2, cy, cz // 2),
                vmem(*plane), vmem(*plane), vmem(*fine), vmem(*fine), vmem(*fine), vmem(*fine),
                vmem(*small), vmem(*small), vmem(*small),
                vmem(2 * REACH + 1, 4, *small), vmem(7, 2 * REACH + 1, *small),
                vmem(*small), vmem(*small), vmem(*small),
                *(vmem(2 * j + 1, *small) for j in NEAR), vmem(2 * MID + 1, *small), vmem(2 * FAR + 1, *small),
                dma((3,)), dma((6,)), dma((6,)), dma((2,)), dma((2 * REACH + 1,)), dma((2, FAR)),
                dma((5, 2 * FAR + 1)), dma((5, 2 * FAR + 1)),
                pltpu.SemaphoreType.REGULAR((7,)),
            ],
            compiler_params=pltpu.CompilerParams(collective_id=0, has_side_effects=True, vmem_limit_bytes=56430000),
        )(initial_states, velocity, diffusivity)
        return (ended + delta[None])[None]

    in_specs = (P("tm", "space", None, None), P(None, "space", None, None), P("space", None, None))
    out_specs = P("tm", "space", None, None)
    return jax.shard_map(shards, mesh=mesh, in_specs=in_specs, out_specs=out_specs, check_vma=False)
```

```python
import functools

import jax
import jax.numpy as jnp
from jax import lax
from jax.experimental import pallas as pl
from jax.experimental.pallas import tpu as pltpu
from jax.sharding import PartitionSpec as P

MESH = pl.DeviceIdType.MESH
REACH = 7
INNER = 3
GREET = 2
FOURTH = 4
NEAR = (1, 2, 3)
MID = 4
FAR = 8
HOPS = NEAR + (MID, FAR)


def seven(diffusivity, vx, vy, vz, spread):
    ak = spread * diffusivity
    hx, hy, hz = 0.5 * vx, 0.5 * vy, 0.5 * vz
    rows = lax.broadcasted_iota(jnp.int32, ak.shape, ak.ndim - 2)
    cols = lax.broadcasted_iota(jnp.int32, ak.shape, ak.ndim - 1)
    zero = jnp.zeros_like(ak)
    return (
        1.0 - 6.0 * ak,
        ak + hx,
        ak - hx,
        jnp.where(rows == 0, zero, ak + hy),
        jnp.where(rows == ak.shape[-2] - 1, zero, ak - hy),
        jnp.where(cols == 0, zero, ak + hz),
        jnp.where(cols == ak.shape[-1] - 1, zero, ak - hz),
    )


def inplane(factors, f):
    c0, _, _, ym, yp, zm, zp = factors
    a, b = f.ndim - 2, f.ndim - 1
    return (
        c0 * f
        + (ym * pltpu.roll(f, 1, a) + yp * pltpu.roll(f, f.shape[a] - 1, a))
        + (zm * pltpu.roll(f, 1, b) + zp * pltpu.roll(f, f.shape[b] - 1, b))
    )


def restrict(work, two):
    rows = two.shape[1]
    both = two[0] + two[1]
    lanes = lax.broadcasted_iota(jnp.int32, (rows // 2, 128), 1)
    place = lax.rem(2 * lanes, 128)
    sides = []
    for h in range(2):
        work[h] = both[:, 128 * h : 128 * (h + 1)]
        half = work[h, pl.ds(0, rows // 2, 2), :] + work[h, pl.ds(1, rows // 2, 2), :]
        half = half + pltpu.roll(half, 127, 1)
        sides.append(jnp.take_along_axis(half, place, axis=1))
    return 0.125 * jnp.where(lanes < 64, sides[0], sides[1])


def kernel(
    nt, ns, init, vel, dif, fine_out, delta_out,
    f_ref, v_ref, k_ref, work, left0, right0, left1, right1, out_low, out_high,
    start_own, start_left, start_right, coef, kap,
    r_ref, u_ref, w_ref, near1, near2, near3, mid, far,
    load_sem, halo_send, halo_recv, coef_send, coef_recv, share_send, hop_send, hop_recv, ready,
):
    t, s = lax.axis_index("tm"), lax.axis_index("space")
    seat = lax.rem(t, FAR)
    group = t - seat
    near = (near1, near2, near3)

    def inside(ds):
        return s + ds < ns if ds > 0 else s + ds >= 0

    def outward(width):
        return [ds for k in range(width, 0, -1) for ds in (k, -k)]

    loads = [
        pltpu.make_async_copy(a, b, load_sem.at[i])
        for i, (a, b) in enumerate(((init.at[0], f_ref), (vel, v_ref), (dif, k_ref)))
    ]
    for copy in loads:
        copy.start()

    for j, slot in zip(NEAR, near):

        @pl.when(t < j)
        def _():
            slot[...] = jnp.zeros_like(slot)

    @pl.when((s < FAR) | (s >= ns - FAR))
    def _():
        for slot in (near1, near2, near3, mid, far, coef):
            slot[...] = jnp.zeros_like(slot)

    @pl.when(s == 0)
    def _():
        for slot in (left0, left1, start_left):
            slot[...] = jnp.zeros_like(slot)

    @pl.when(s == ns - 1)
    def _():
        for slot in (right0, right1, start_right):
            slot[...] = jnp.zeros_like(slot)

    barrier = pltpu.get_barrier_semaphore()
    for ds in reversed(outward(GREET)):

        @pl.when(inside(ds))
        def _():
            pl.semaphore_signal(barrier, inc=1, device_id=(t, s + ds), device_id_type=MESH)

    for j in range(1, FAR + 1):

        @pl.when((t + j < nt) if j in HOPS else (seat + j < FAR))
        def _():
            pl.semaphore_signal(barrier, inc=1, device_id=(t + j, s), device_id_type=MESH)

    for copy in loads:
        copy.wait()
    fine0 = seven(k_ref[0], v_ref[0, 0], v_ref[1, 0], v_ref[2, 0], 1.0)
    fine1 = seven(k_ref[1], v_ref[0, 1], v_ref[1, 1], v_ref[2, 1], 1.0)

    def partial(a, b):
        return inplane(fine0, a) + fine0[2] * b, inplane(fine1, b) + fine1[1] * a

    pa, pb = partial(f_ref[0], f_ref[1])
    out_low[0], out_low[1] = fine0[1], pa
    out_high[0], out_high[1] = fine1[2], pb

    start = restrict(work.at[0], f_ref)
    start_own[...] = start
    coarse = [restrict(work.at[1 + i], v_ref[i]) for i in range(3)]
    coarse.append(restrict(work.at[4], k_ref))
    for i in range(4):
        coef[REACH, i] = coarse[i]

    senders = sum(jnp.where((t if j in HOPS else seat) >= j, 1, 0) for j in range(1, FAR + 1))
    beside = jnp.minimum(s, GREET) + jnp.minimum(ns - 1 - s, GREET)
    pl.semaphore_wait(barrier, beside + senders)

    def remote(src, dst, send, recv, tt, ds):
        return pltpu.make_async_remote_copy(
            src_ref=src, dst_ref=dst, send_sem=send, recv_sem=recv, device_id=(tt, s + ds), device_id_type=MESH
        )

    def beside_do(pair, what):
        down, up = pair

        @pl.when(s > 0)
        def _():
            if what == "start":
                down.start()
            elif what == "recv":
                up.wait_recv()
            else:
                down.wait_send()

        @pl.when(s < ns - 1)
        def _():
            if what == "start":
                up.start()
            elif what == "recv":
                down.wait_recv()
            else:
                up.wait_send()

    halo0 = [
        remote(f_ref.at[0], right0, halo_send.at[0], halo_recv.at[0], t, -1),
        remote(f_ref.at[1], left0, halo_send.at[1], halo_recv.at[1], t, 1),
    ]
    halo1 = [
        remote(out_low, right1, halo_send.at[4], halo_recv.at[4], t, -1),
        remote(out_high, left1, halo_send.at[5], halo_recv.at[5], t, 1),
    ]
    halo_c = [
        remote(start_own, start_right, halo_send.at[2], halo_recv.at[2], t, -1),
        remote(start_own, start_left, halo_send.at[3], halo_recv.at[3], t, 1),
    ]
    def reach(off):
        return (s + off >= 0) & (s + off < ns)

    near_off = jnp.where(seat < GREET, seat - GREET, seat - GREET + 1)
    inner = (seat < 2 * INNER, jnp.where(seat < 2 * GREET, near_off, jnp.where(seat == 2 * GREET, -INNER, INNER)))
    inner_first = (seat < 2 * GREET, inner[1])
    inner_last = ((seat >= 2 * GREET) & (seat < 2 * INNER), inner[1])
    outer = (group > 0, jnp.where(seat < REACH - INNER, seat - REACH, seat))

    def fetch(who, i):
        needed, off = who

        @pl.when(needed & reach(-off))
        def _():
            there = REACH + off
            remote(coef.at[REACH], coef.at[there], coef_send.at[i], coef_recv.at[there], t, -off).start()

    def fetched(who, i):
        needed, off = who

        @pl.when(needed & reach(-off))
        def _():
            pltpu.make_async_copy(coef.at[REACH], coef.at[REACH], coef_send.at[i]).wait()

    def hand_on(who, i):
        needed, off = who

        @pl.when(needed & reach(off))
        def _():
            here = REACH + off
            pltpu.make_async_copy(coef.at[here], coef.at[here], coef_recv.at[here]).wait()
            for turn in (4, 3, 5, 2, 6, 1, 7):
                to = group + lax.rem(seat + turn, FAR)
                remote(coef.at[here], coef.at[here], share_send.at[i, turn], coef_recv.at[here], to, 0).start()

    def handed_on(who, i):
        needed, off = who

        @pl.when(needed & reach(off))
        def _():
            for turn in range(1, FAR):
                pltpu.make_async_copy(coef.at[REACH], coef.at[REACH], share_send.at[i, turn]).wait()

    def handed(who, offs):
        needed, off = who
        for o in offs:

            @pl.when(inside(o) & (jnp.logical_not(needed) | (off != o)))
            def _():
                pltpu.make_async_copy(coef.at[REACH + o], coef.at[REACH + o], coef_recv.at[REACH + o]).wait()

    beside_do(halo0, "start")
    fetch(inner_first, 0)
    beside_do(halo1, "start")
    beside_do(halo_c, "start")
    def tell(i, j):
        @pl.when(t >= j)
        def _():
            pl.semaphore_signal(ready.at[i], inc=1, device_id=(t - j, s), device_id_type=MESH)

    def word(i, width):
        for ds in (width, -width):

            @pl.when(inside(ds))
            def _():
                pl.semaphore_signal(ready.at[i], inc=1, device_id=(t, s + ds), device_id_type=MESH)

    def heard(i, width):
        pl.semaphore_wait(ready.at[i], jnp.where(inside(width), 1, 0) + jnp.where(inside(-width), 1, 0))

    word(7, GREET)
    for i, j in enumerate(HOPS):
        if j <= GREET:
            tell(i, j)
    for j in range(1, FAR):

        @pl.when(seat >= j)
        def _():
            pl.semaphore_signal(ready.at[5], inc=1, device_id=(t - j, s), device_id_type=MESH)

    heard(7, GREET)
    fetch(inner_last, 0)
    for i, j in enumerate(HOPS):
        if GREET < j <= FOURTH:
            tell(i, j)

    @pl.when(group > 0)
    def _():
        word(6, FOURTH)

    @pl.when(seat < FAR - 1)
    def _():
        pl.semaphore_wait(ready.at[5], FAR - 1 - seat)

    hand_on(inner, 0)

    one = jnp.float32(1.0)
    own = seven(coarse[3], coarse[0], coarse[1], coarse[2], 0.5)
    beside_do(halo_c, "recv")
    stepped = inplane(own, start) + (own[1] * start_left[...] + own[2] * start_right[...])
    beside_do(halo0, "recv")
    a = pa + fine0[1] * left0[...]
    b = pb + fine1[2] * right0[...]
    pa, pb = partial(a, b)
    beside_do(halo1, "recv")
    fine_out[0] = pa + fine0[1] * (left1[1] + left1[0] * f_ref[0])
    fine_out[1] = pb + fine1[2] * (right1[1] + right1[0] * f_ref[1])
    end = restrict(work.at[0], fine_out)
    r_ref[...] = end - jnp.where(t == 0, 0.0, one) * stepped

    def each(width, slot, sem, mirrored):
        low, high = jnp.minimum(s, width), jnp.minimum(ns - 1 - s, width)
        if mirrored:
            low, high = high, low

        def one_of(i, _):
            pltpu.make_async_copy(slot(i), slot(i), sem(i)).wait()
            return 0

        lax.fori_loop(width - low, width + high + 1, one_of, 0)

    def hop(number, dt, src, slot):
        @pl.when(t + dt < nt)
        def _():
            pl.semaphore_wait(ready.at[number], 1)

            def send(ds):
                i = dt - ds
                remote(src, slot.at[i], hop_send.at[number, i], hop_recv.at[number, i], t + dt, ds).start()

            for ds in outward(dt):
                pl.when(inside(ds))(functools.partial(send, ds))
            send(0)

    def arrived(number, dt, slot):
        @pl.when(t >= dt)
        def _():
            each(dt, lambda i: slot.at[i], lambda i: hop_recv.at[number, i], False)

    def sent(number, dt, slot):
        @pl.when(t + dt < nt)
        def _():
            each(dt, lambda i: slot.at[i], lambda i: hop_send.at[number, i], True)

    for i, j in enumerate(NEAR):
        hop(i, j, r_ref, near[i])

    def factors_of(first, last):
        for i in range(first, last):
            factors = seven(coef[i, 3], coef[i, 0], coef[i, 1], coef[i, 2], 0.5)
            for n in range(7):
                kap[n, i] = factors[n]

    low, high = REACH - INNER, REACH + INNER + 1
    @pl.when(group > 0)
    def _():
        heard(6, FOURTH)
        tell(len(HOPS) - 1, FAR)

    fetch(outer, 1)
    handed(inner, [o for o in range(-INNER, INNER + 1) if o])
    factors_of(low, high)

    def coarse_step(v):
        w = (v.shape[0] - 3) // 2
        factors = [kap[n, REACH - w : REACH + w + 1] for n in range(7)]
        return inplane(factors, v[1:-1]) + (factors[1] * v[:-2] + factors[2] * v[2:])

    for i, j in enumerate(NEAR):
        arrived(i, j, near[i])
    v = near3[...]
    v = coarse_step(v) + near2[...]
    v = coarse_step(v) + near1[...]
    u_ref[...] = coarse_step(v)[0] + r_ref[...]

    hop(3, MID, u_ref, mid)
    hand_on(outer, 1)
    arrived(3, MID, mid)

    @pl.when(t >= MID)
    def _():
        v = mid[...]
        for _ in range(MID):
            v = coarse_step(v)
        w_ref[...] = v[0] + u_ref[...]

    @pl.when(t < MID)
    def _():
        w_ref[...] = u_ref[...]

    hop(4, FAR, w_ref, far)

    for pair in (halo0, halo_c, halo1):
        beside_do(pair, "send")
    fetched(inner, 0)
    fetched(outer, 1)
    handed_on(inner, 0)
    handed_on(outer, 1)
    for i, j in enumerate(NEAR):
        sent(i, j, near[i])
    sent(3, MID, mid)

    @pl.when(t >= FAR)
    def _():
        handed(outer, [o for o in range(-REACH, REACH + 1) if abs(o) > INNER])
        factors_of(0, low)
        factors_of(high, 2 * REACH + 1)

    arrived(4, FAR, far)

    def finish(c):
        d = c - end
        lanes = lax.broadcasted_iota(jnp.int32, d.shape, 1)
        for h in range(2):
            wide = jnp.take_along_axis(d, lanes // 2 + 64 * h, axis=1)
            for i in range(2):
                work[0, h, pl.ds(i, d.shape[0], 2), :] = wide
            delta_out[:, 128 * h : 128 * (h + 1)] = work[0, h]

    @pl.when(t >= FAR)
    def _():
        v = far[...]
        for _ in range(FAR):
            v = coarse_step(v)
        finish(v[0] + w_ref[...])

    @pl.when(t < FAR)
    def _():
        finish(w_ref[...])

    sent(4, FAR, far)


def solution(mesh):
    nt, ns = mesh.shape["tm"], mesh.shape["space"]

    def shards(initial_states, velocity, diffusivity):
        _, planes, cy, cz = initial_states.shape
        fine = (planes, cy, cz)
        plane, small = (cy, cz), (cy // 2, cz // 2)

        def vmem(*shape):
            return pltpu.VMEM(shape, jnp.float32)

        dma = pltpu.SemaphoreType.DMA
        ended, delta = pl.pallas_call(
            lambda *refs: kernel(nt, ns, *refs),
            out_shape=(jax.ShapeDtypeStruct(fine, jnp.float32), jax.ShapeDtypeStruct(plane, jnp.float32)),
            in_specs=[pl.BlockSpec(memory_space=pltpu.HBM)] * 3,
            out_specs=(pl.BlockSpec(memory_space=pltpu.VMEM),) * 2,
            scratch_shapes=[
                vmem(*fine), vmem(3, *fine), vmem(*fine), vmem(5, 2, cy, cz // 2),
                vmem(*plane), vmem(*plane), vmem(*fine), vmem(*fine), vmem(*fine), vmem(*fine),
                vmem(*small), vmem(*small), vmem(*small),
                vmem(2 * REACH + 1, 4, *small), vmem(7, 2 * REACH + 1, *small),
                vmem(*small), vmem(*small), vmem(*small),
                *(vmem(2 * j + 1, *small) for j in NEAR), vmem(2 * MID + 1, *small), vmem(2 * FAR + 1, *small),
                dma((3,)), dma((6,)), dma((6,)), dma((2,)), dma((2 * REACH + 1,)), dma((2, FAR)),
                dma((5, 2 * FAR + 1)), dma((5, 2 * FAR + 1)),
                pltpu.SemaphoreType.REGULAR((8,)),
            ],
            compiler_params=pltpu.CompilerParams(collective_id=0, has_side_effects=True, vmem_limit_bytes=56430000),
        )(initial_states, velocity, diffusivity)
        return (ended + delta[None])[None]

    in_specs = (P("tm", "space", None, None), P(None, "space", None, None), P("space", None, None))
    out_specs = P("tm", "space", None, None)
    return jax.shard_map(shards, mesh=mesh, in_specs=in_specs, out_specs=out_specs, check_vma=False)
```

```python
import functools

import jax
import jax.numpy as jnp
from jax import lax
from jax.experimental import pallas as pl
from jax.experimental.pallas import tpu as pltpu
from jax.sharding import PartitionSpec as P

MESH = pl.DeviceIdType.MESH
REACH = 7
INNER = 3
GREET = 2
FOURTH = 4
NEAR = (1, 2, 3)
MID = 4
FAR = 8
HOPS = NEAR + (MID, FAR)


def seven(diffusivity, vx, vy, vz, spread):
    ak = spread * diffusivity
    hx, hy, hz = 0.5 * vx, 0.5 * vy, 0.5 * vz
    rows = lax.broadcasted_iota(jnp.int32, ak.shape, ak.ndim - 2)
    cols = lax.broadcasted_iota(jnp.int32, ak.shape, ak.ndim - 1)
    zero = jnp.zeros_like(ak)
    return (
        1.0 - 6.0 * ak,
        ak + hx,
        ak - hx,
        jnp.where(rows == 0, zero, ak + hy),
        jnp.where(rows == ak.shape[-2] - 1, zero, ak - hy),
        jnp.where(cols == 0, zero, ak + hz),
        jnp.where(cols == ak.shape[-1] - 1, zero, ak - hz),
    )


def inplane(factors, f):
    c0, _, _, ym, yp, zm, zp = factors
    a, b = f.ndim - 2, f.ndim - 1
    return (
        c0 * f
        + (ym * pltpu.roll(f, 1, a) + yp * pltpu.roll(f, f.shape[a] - 1, a))
        + (zm * pltpu.roll(f, 1, b) + zp * pltpu.roll(f, f.shape[b] - 1, b))
    )


def restrict(work, two):
    rows = two.shape[1]
    both = two[0] + two[1]
    lanes = lax.broadcasted_iota(jnp.int32, (rows // 2, 128), 1)
    place = lax.rem(2 * lanes, 128)
    sides = []
    for h in range(2):
        work[h] = both[:, 128 * h : 128 * (h + 1)]
        half = work[h, pl.ds(0, rows // 2, 2), :] + work[h, pl.ds(1, rows // 2, 2), :]
        half = half + pltpu.roll(half, 127, 1)
        sides.append(jnp.take_along_axis(half, place, axis=1))
    return 0.125 * jnp.where(lanes < 64, sides[0], sides[1])


def kernel(
    nt, ns, init, vel, dif, fine_out, delta_out,
    f_ref, v_ref, k_ref, work, left0, right0, left1, right1, out_low, out_high,
    start_own, start_left, start_right, coef, kap,
    r_ref, u_ref, w_ref, near1, near2, near3, mid, far,
    load_sem, halo_send, halo_recv, coef_send, coef_recv, share_send, hop_send, hop_recv, ready,
):
    t, s = lax.axis_index("tm"), lax.axis_index("space")
    seat = lax.rem(t, FAR)
    group = t - seat
    near = (near1, near2, near3)

    def inside(ds):
        return s + ds < ns if ds > 0 else s + ds >= 0

    def outward(width):
        return [ds for k in range(width, 0, -1) for ds in (k, -k)]

    loads = [
        pltpu.make_async_copy(a, b, load_sem.at[i])
        for i, (a, b) in enumerate(((init.at[0], f_ref), (vel, v_ref), (dif, k_ref)))
    ]
    for copy in loads:
        copy.start()

    for j, slot in zip(NEAR, near):

        @pl.when(t < j)
        def _():
            slot[...] = jnp.zeros_like(slot)

    @pl.when((s < FAR) | (s >= ns - FAR))
    def _():
        for slot in (near1, near2, near3, mid, far, coef):
            slot[...] = jnp.zeros_like(slot)

    @pl.when(s == 0)
    def _():
        for slot in (left0, left1, start_left):
            slot[...] = jnp.zeros_like(slot)

    @pl.when(s == ns - 1)
    def _():
        for slot in (right0, right1, start_right):
            slot[...] = jnp.zeros_like(slot)

    barrier = pltpu.get_barrier_semaphore()
    for ds in reversed(outward(GREET)):

        @pl.when(inside(ds))
        def _():
            pl.semaphore_signal(barrier, inc=1, device_id=(t, s + ds), device_id_type=MESH)

    for j in range(1, FAR + 1):

        @pl.when((t + j < nt) if j in HOPS else (seat + j < FAR))
        def _():
            pl.semaphore_signal(barrier, inc=1, device_id=(t + j, s), device_id_type=MESH)

    for copy in loads:
        copy.wait()
    fine0 = seven(k_ref[0], v_ref[0, 0], v_ref[1, 0], v_ref[2, 0], 1.0)
    fine1 = seven(k_ref[1], v_ref[0, 1], v_ref[1, 1], v_ref[2, 1], 1.0)

    def partial(a, b):
        return inplane(fine0, a) + fine0[2] * b, inplane(fine1, b) + fine1[1] * a

    pa, pb = partial(f_ref[0], f_ref[1])
    out_low[0], out_low[1] = fine0[1], pa
    out_high[0], out_high[1] = fine1[2], pb

    start = restrict(work.at[0], f_ref)
    start_own[...] = start
    coarse = [restrict(work.at[1 + i], v_ref[i]) for i in range(3)]
    coarse.append(restrict(work.at[4], k_ref))
    for i in range(4):
        coef[REACH, i] = coarse[i]

    senders = sum(jnp.where((t if j in HOPS else seat) >= j, 1, 0) for j in range(1, FAR + 1))
    beside = jnp.minimum(s, GREET) + jnp.minimum(ns - 1 - s, GREET)
    pl.semaphore_wait(barrier, beside + senders)

    def remote(src, dst, send, recv, tt, ds):
        return pltpu.make_async_remote_copy(
            src_ref=src, dst_ref=dst, send_sem=send, recv_sem=recv, device_id=(tt, s + ds), device_id_type=MESH
        )

    def beside_do(pair, what):
        down, up = pair

        @pl.when(s > 0)
        def _():
            if what == "start":
                down.start()
            elif what == "recv":
                up.wait_recv()
            else:
                down.wait_send()

        @pl.when(s < ns - 1)
        def _():
            if what == "start":
                up.start()
            elif what == "recv":
                down.wait_recv()
            else:
                up.wait_send()

    halo0 = [
        remote(f_ref.at[0], right0, halo_send.at[0], halo_recv.at[0], t, -1),
        remote(f_ref.at[1], left0, halo_send.at[1], halo_recv.at[1], t, 1),
    ]
    halo1 = [
        remote(out_low, right1, halo_send.at[4], halo_recv.at[4], t, -1),
        remote(out_high, left1, halo_send.at[5], halo_recv.at[5], t, 1),
    ]
    halo_c = [
        remote(start_own, start_right, halo_send.at[2], halo_recv.at[2], t, -1),
        remote(start_own, start_left, halo_send.at[3], halo_recv.at[3], t, 1),
    ]
    def reach(off):
        return (s + off >= 0) & (s + off < ns)

    near_off = jnp.where(seat < GREET, seat - GREET, seat - GREET + 1)
    inner = (seat < 2 * INNER, jnp.where(seat < 2 * GREET, near_off, jnp.where(seat == 2 * GREET, -INNER, INNER)))
    inner_first = (seat < 2 * GREET, inner[1])
    inner_last = ((seat >= 2 * GREET) & (seat < 2 * INNER), inner[1])
    outer = (group > 0, jnp.where(seat < REACH - INNER, seat - REACH, seat))

    def fetch(who, i):
        needed, off = who

        @pl.when(needed & reach(-off))
        def _():
            there = REACH + off
            remote(coef.at[REACH], coef.at[there], coef_send.at[i], coef_recv.at[there], t, -off).start()

    def fetched(who, i):
        needed, off = who

        @pl.when(needed & reach(-off))
        def _():
            pltpu.make_async_copy(coef.at[REACH], coef.at[REACH], coef_send.at[i]).wait()

    def hand_on(who, i):
        needed, off = who

        @pl.when(needed & reach(off))
        def _():
            here = REACH + off
            pltpu.make_async_copy(coef.at[here], coef.at[here], coef_recv.at[here]).wait()
            for turn in (4, 3, 5, 2, 6, 1, 7):
                to = group + lax.rem(seat + turn, FAR)
                remote(coef.at[here], coef.at[here], share_send.at[i, turn], coef_recv.at[here], to, 0).start()

    def handed_on(who, i):
        needed, off = who

        @pl.when(needed & reach(off))
        def _():
            for turn in range(1, FAR):
                pltpu.make_async_copy(coef.at[REACH], coef.at[REACH], share_send.at[i, turn]).wait()

    def handed(who, offs):
        needed, off = who
        for o in offs:

            @pl.when(inside(o) & (jnp.logical_not(needed) | (off != o)))
            def _():
                pltpu.make_async_copy(coef.at[REACH + o], coef.at[REACH + o], coef_recv.at[REACH + o]).wait()

    beside_do(halo0, "start")
    fetch(inner_first, 0)
    beside_do(halo1, "start")
    beside_do(halo_c, "start")
    def tell(i, j):
        @pl.when(t >= j)
        def _():
            pl.semaphore_signal(ready.at[i], inc=1, device_id=(t - j, s), device_id_type=MESH)

    def word(i, width):
        for ds in (width, -width):

            @pl.when(inside(ds))
            def _():
                pl.semaphore_signal(ready.at[i], inc=1, device_id=(t, s + ds), device_id_type=MESH)

    def heard(i, width):
        pl.semaphore_wait(ready.at[i], jnp.where(inside(width), 1, 0) + jnp.where(inside(-width), 1, 0))

    word(7, GREET)
    for i, j in enumerate(HOPS):
        if j <= GREET:
            tell(i, j)
    for j in range(1, FAR):

        @pl.when(seat >= j)
        def _():
            pl.semaphore_signal(ready.at[5], inc=1, device_id=(t - j, s), device_id_type=MESH)

    heard(7, GREET)
    fetch(inner_last, 0)
    for i, j in enumerate(HOPS):
        if GREET < j <= FOURTH:
            tell(i, j)

    @pl.when(group > 0)
    def _():
        word(6, FOURTH)

    @pl.when(seat < FAR - 1)
    def _():
        pl.semaphore_wait(ready.at[5], FAR - 1 - seat)

    hand_on(inner_first, 0)

    one = jnp.float32(1.0)
    own = seven(coarse[3], coarse[0], coarse[1], coarse[2], 0.5)
    beside_do(halo_c, "recv")
    stepped = inplane(own, start) + (own[1] * start_left[...] + own[2] * start_right[...])
    beside_do(halo0, "recv")
    a = pa + fine0[1] * left0[...]
    b = pb + fine1[2] * right0[...]
    pa, pb = partial(a, b)
    beside_do(halo1, "recv")
    fine_out[0] = pa + fine0[1] * (left1[1] + left1[0] * f_ref[0])
    fine_out[1] = pb + fine1[2] * (right1[1] + right1[0] * f_ref[1])
    end = restrict(work.at[0], fine_out)
    r_ref[...] = end - jnp.where(t == 0, 0.0, one) * stepped

    def each(width, slot, sem, mirrored):
        low, high = jnp.minimum(s, width), jnp.minimum(ns - 1 - s, width)
        if mirrored:
            low, high = high, low

        def one_of(i, _):
            pltpu.make_async_copy(slot(i), slot(i), sem(i)).wait()
            return 0

        lax.fori_loop(width - low, width + high + 1, one_of, 0)

    def hop(number, dt, src, slot):
        @pl.when(t + dt < nt)
        def _():
            pl.semaphore_wait(ready.at[number], 1)

            def send(ds):
                i = dt - ds
                remote(src, slot.at[i], hop_send.at[number, i], hop_recv.at[number, i], t + dt, ds).start()

            for ds in outward(dt):
                pl.when(inside(ds))(functools.partial(send, ds))
            send(0)

    def arrived(number, dt, slot):
        @pl.when(t >= dt)
        def _():
            each(dt, lambda i: slot.at[i], lambda i: hop_recv.at[number, i], False)

    def sent(number, dt, slot):
        @pl.when(t + dt < nt)
        def _():
            each(dt, lambda i: slot.at[i], lambda i: hop_send.at[number, i], True)

    for i, j in enumerate(NEAR):
        hop(i, j, r_ref, near[i])

    def factors_of(first, last):
        for i in range(first, last):
            factors = seven(coef[i, 3], coef[i, 0], coef[i, 1], coef[i, 2], 0.5)
            for n in range(7):
                kap[n, i] = factors[n]

    low, high = REACH - INNER, REACH + INNER + 1
    @pl.when(group > 0)
    def _():
        heard(6, FOURTH)
        tell(len(HOPS) - 1, FAR)

    fetch(outer, 1)
    hand_on(inner_last, 0)
    handed(inner, [o for o in range(-GREET, GREET + 1) if o])
    factors_of(low + 1, high - 1)

    def coarse_step(v):
        w = (v.shape[0] - 3) // 2
        factors = [kap[n, REACH - w : REACH + w + 1] for n in range(7)]
        return inplane(factors, v[1:-1]) + (factors[1] * v[:-2] + factors[2] * v[2:])

    for i, j in enumerate(NEAR):
        arrived(i, j, near[i])
    v = near3[...]
    v = coarse_step(v) + near2[...]
    v = coarse_step(v) + near1[...]
    u_ref[...] = coarse_step(v)[0] + r_ref[...]

    hop(3, MID, u_ref, mid)
    handed(inner, [-INNER, INNER])
    factors_of(low, low + 1)
    factors_of(high - 1, high)
    hand_on(outer, 1)
    arrived(3, MID, mid)

    @pl.when(t >= MID)
    def _():
        v = mid[...]
        for _ in range(MID):
            v = coarse_step(v)
        w_ref[...] = v[0] + u_ref[...]

    @pl.when(t < MID)
    def _():
        w_ref[...] = u_ref[...]

    hop(4, FAR, w_ref, far)

    for pair in (halo0, halo_c, halo1):
        beside_do(pair, "send")
    fetched(inner, 0)
    fetched(outer, 1)
    handed_on(inner, 0)
    handed_on(outer, 1)
    for i, j in enumerate(NEAR):
        sent(i, j, near[i])
    sent(3, MID, mid)

    @pl.when(t >= FAR)
    def _():
        handed(outer, [o for o in range(-REACH, REACH + 1) if abs(o) > INNER])
        factors_of(0, low)
        factors_of(high, 2 * REACH + 1)

    arrived(4, FAR, far)

    def finish(c):
        d = c - end
        lanes = lax.broadcasted_iota(jnp.int32, d.shape, 1)
        for h in range(2):
            wide = jnp.take_along_axis(d, lanes // 2 + 64 * h, axis=1)
            for i in range(2):
                work[0, h, pl.ds(i, d.shape[0], 2), :] = wide
            delta_out[:, 128 * h : 128 * (h + 1)] = work[0, h]

    @pl.when(t >= FAR)
    def _():
        v = far[...]
        for _ in range(FAR):
            v = coarse_step(v)
        finish(v[0] + w_ref[...])

    @pl.when(t < FAR)
    def _():
        finish(w_ref[...])

    sent(4, FAR, far)


def solution(mesh):
    nt, ns = mesh.shape["tm"], mesh.shape["space"]

    def shards(initial_states, velocity, diffusivity):
        _, planes, cy, cz = initial_states.shape
        fine = (planes, cy, cz)
        plane, small = (cy, cz), (cy // 2, cz // 2)

        def vmem(*shape):
            return pltpu.VMEM(shape, jnp.float32)

        dma = pltpu.SemaphoreType.DMA
        ended, delta = pl.pallas_call(
            lambda *refs: kernel(nt, ns, *refs),
            out_shape=(jax.ShapeDtypeStruct(fine, jnp.float32), jax.ShapeDtypeStruct(plane, jnp.float32)),
            in_specs=[pl.BlockSpec(memory_space=pltpu.HBM)] * 3,
            out_specs=(pl.BlockSpec(memory_space=pltpu.VMEM),) * 2,
            scratch_shapes=[
                vmem(*fine), vmem(3, *fine), vmem(*fine), vmem(5, 2, cy, cz // 2),
                vmem(*plane), vmem(*plane), vmem(*fine), vmem(*fine), vmem(*fine), vmem(*fine),
                vmem(*small), vmem(*small), vmem(*small),
                vmem(2 * REACH + 1, 4, *small), vmem(7, 2 * REACH + 1, *small),
                vmem(*small), vmem(*small), vmem(*small),
                *(vmem(2 * j + 1, *small) for j in NEAR), vmem(2 * MID + 1, *small), vmem(2 * FAR + 1, *small),
                dma((3,)), dma((6,)), dma((6,)), dma((2,)), dma((2 * REACH + 1,)), dma((2, FAR)),
                dma((5, 2 * FAR + 1)), dma((5, 2 * FAR + 1)),
                pltpu.SemaphoreType.REGULAR((8,)),
            ],
            compiler_params=pltpu.CompilerParams(collective_id=0, has_side_effects=True, vmem_limit_bytes=56430000),
        )(initial_states, velocity, diffusivity)
        return (ended + delta[None])[None]

    in_specs = (P("tm", "space", None, None), P(None, "space", None, None), P("space", None, None))
    out_specs = P("tm", "space", None, None)
    return jax.shard_map(shards, mesh=mesh, in_specs=in_specs, out_specs=out_specs, check_vma=False)
```

```python
import functools

import jax
import jax.numpy as jnp
from jax import lax
from jax.experimental import pallas as pl
from jax.experimental.pallas import tpu as pltpu
from jax.sharding import PartitionSpec as P

MESH = pl.DeviceIdType.MESH
REACH = 7
INNER = 3
GREET = 2
FOURTH = 4
NEAR = (1, 2, 3)
MID = 4
FAR = 8
HOPS = NEAR + (MID, FAR)


def seven(diffusivity, vx, vy, vz, spread):
    ak = spread * diffusivity
    hx, hy, hz = 0.5 * vx, 0.5 * vy, 0.5 * vz
    rows = lax.broadcasted_iota(jnp.int32, ak.shape, ak.ndim - 2)
    cols = lax.broadcasted_iota(jnp.int32, ak.shape, ak.ndim - 1)
    zero = jnp.zeros_like(ak)
    return (
        1.0 - 6.0 * ak,
        ak + hx,
        ak - hx,
        jnp.where(rows == 0, zero, ak + hy),
        jnp.where(rows == ak.shape[-2] - 1, zero, ak - hy),
        jnp.where(cols == 0, zero, ak + hz),
        jnp.where(cols == ak.shape[-1] - 1, zero, ak - hz),
    )


def inplane(factors, f):
    c0, _, _, ym, yp, zm, zp = factors
    a, b = f.ndim - 2, f.ndim - 1
    return (
        c0 * f
        + (ym * pltpu.roll(f, 1, a) + yp * pltpu.roll(f, f.shape[a] - 1, a))
        + (zm * pltpu.roll(f, 1, b) + zp * pltpu.roll(f, f.shape[b] - 1, b))
    )


def restrict(work, two):
    rows = two.shape[1]
    both = two[0] + two[1]
    lanes = lax.broadcasted_iota(jnp.int32, (rows // 2, 128), 1)
    place = lax.rem(2 * lanes, 128)
    sides = []
    for h in range(2):
        work[h] = both[:, 128 * h : 128 * (h + 1)]
        half = work[h, pl.ds(0, rows // 2, 2), :] + work[h, pl.ds(1, rows // 2, 2), :]
        half = half + pltpu.roll(half, 127, 1)
        sides.append(jnp.take_along_axis(half, place, axis=1))
    return 0.125 * jnp.where(lanes < 64, sides[0], sides[1])


def kernel(
    nt, ns, init, vel, dif, fine_out, delta_out,
    f_ref, v_ref, k_ref, work, left0, right0, left1, right1, out_low, out_high,
    start_own, start_left, start_right, coef, kap,
    r_ref, u_ref, w_ref, near1, near2, near3, mid, far,
    load_sem, halo_send, halo_recv, coef_send, coef_recv, share_send, hop_send, hop_recv, ready,
):
    t, s = lax.axis_index("tm"), lax.axis_index("space")
    seat = lax.rem(t, FAR)
    group = t - seat
    near = (near1, near2, near3)

    def inside(ds):
        return s + ds < ns if ds > 0 else s + ds >= 0

    def outward(width):
        return [ds for k in range(width, 0, -1) for ds in (k, -k)]

    loads = [
        pltpu.make_async_copy(a, b, load_sem.at[i])
        for i, (a, b) in enumerate(((init.at[0], f_ref), (vel, v_ref), (dif, k_ref)))
    ]
    for copy in loads:
        copy.start()

    for j, slot in zip(NEAR, near):

        @pl.when(t < j)
        def _():
            slot[...] = jnp.zeros_like(slot)

    @pl.when((s < FAR) | (s >= ns - FAR))
    def _():
        for slot in (near1, near2, near3, mid, far, coef):
            slot[...] = jnp.zeros_like(slot)

    @pl.when(s == 0)
    def _():
        for slot in (left0, left1, start_left):
            slot[...] = jnp.zeros_like(slot)

    @pl.when(s == ns - 1)
    def _():
        for slot in (right0, right1, start_right):
            slot[...] = jnp.zeros_like(slot)

    barrier = pltpu.get_barrier_semaphore()
    for ds in reversed(outward(GREET)):

        @pl.when(inside(ds))
        def _():
            pl.semaphore_signal(barrier, inc=1, device_id=(t, s + ds), device_id_type=MESH)

    for j in range(1, FAR + 1):

        @pl.when((t + j < nt) if j in HOPS else (seat + j < FAR))
        def _():
            pl.semaphore_signal(barrier, inc=1, device_id=(t + j, s), device_id_type=MESH)

    for copy in loads:
        copy.wait()
    fine0 = seven(k_ref[0], v_ref[0, 0], v_ref[1, 0], v_ref[2, 0], 1.0)
    fine1 = seven(k_ref[1], v_ref[0, 1], v_ref[1, 1], v_ref[2, 1], 1.0)

    def partial(a, b):
        return inplane(fine0, a) + fine0[2] * b, inplane(fine1, b) + fine1[1] * a

    pa, pb = partial(f_ref[0], f_ref[1])
    out_low[0], out_low[1] = fine0[1], pa
    out_high[0], out_high[1] = fine1[2], pb

    start = restrict(work.at[0], f_ref)
    start_own[...] = start
    coarse = [restrict(work.at[1 + i], v_ref[i]) for i in range(3)]
    coarse.append(restrict(work.at[4], k_ref))
    for i in range(4):
        coef[REACH, i] = coarse[i]

    senders = sum(jnp.where((t if j in HOPS else seat) >= j, 1, 0) for j in range(1, FAR + 1))
    beside = jnp.minimum(s, GREET) + jnp.minimum(ns - 1 - s, GREET)
    pl.semaphore_wait(barrier, beside + senders)

    def remote(src, dst, send, recv, tt, ds):
        return pltpu.make_async_remote_copy(
            src_ref=src, dst_ref=dst, send_sem=send, recv_sem=recv, device_id=(tt, s + ds), device_id_type=MESH
        )

    def beside_do(pair, what):
        down, up = pair

        @pl.when(s > 0)
        def _():
            if what == "start":
                down.start()
            elif what == "recv":
                up.wait_recv()
            else:
                down.wait_send()

        @pl.when(s < ns - 1)
        def _():
            if what == "start":
                up.start()
            elif what == "recv":
                down.wait_recv()
            else:
                up.wait_send()

    halo0 = [
        remote(f_ref.at[0], right0, halo_send.at[0], halo_recv.at[0], t, -1),
        remote(f_ref.at[1], left0, halo_send.at[1], halo_recv.at[1], t, 1),
    ]
    halo1 = [
        remote(out_low, right1, halo_send.at[4], halo_recv.at[4], t, -1),
        remote(out_high, left1, halo_send.at[5], halo_recv.at[5], t, 1),
    ]
    halo_c = [
        remote(start_own, start_right, halo_send.at[2], halo_recv.at[2], t, -1),
        remote(start_own, start_left, halo_send.at[3], halo_recv.at[3], t, 1),
    ]
    def reach(off):
        return (s + off >= 0) & (s + off < ns)

    near_off = jnp.where(seat < GREET, seat - GREET, seat - GREET + 1)
    inner = (seat < 2 * INNER, jnp.where(seat < 2 * GREET, near_off, jnp.where(seat == 2 * GREET, -INNER, INNER)))
    inner_first = (seat < 2 * GREET, inner[1])
    inner_last = ((seat >= 2 * GREET) & (seat < 2 * INNER), inner[1])
    outer = (group > 0, jnp.where(seat < REACH - INNER, seat - REACH, seat))

    def fetch(who, i):
        needed, off = who

        @pl.when(needed & reach(-off))
        def _():
            there = REACH + off
            remote(coef.at[REACH], coef.at[there], coef_send.at[i], coef_recv.at[there], t, -off).start()

    def fetched(who, i):
        needed, off = who

        @pl.when(needed & reach(-off))
        def _():
            pltpu.make_async_copy(coef.at[REACH], coef.at[REACH], coef_send.at[i]).wait()

    def hand_on(who, i):
        needed, off = who

        @pl.when(needed & reach(off))
        def _():
            here = REACH + off
            pltpu.make_async_copy(coef.at[here], coef.at[here], coef_recv.at[here]).wait()
            for turn in (4, 3, 5, 2, 6, 1, 7):
                to = group + lax.rem(seat + turn, FAR)
                remote(coef.at[here], coef.at[here], share_send.at[i, turn], coef_recv.at[here], to, 0).start()

    def handed_on(who, i):
        needed, off = who

        @pl.when(needed & reach(off))
        def _():
            for turn in range(1, FAR):
                pltpu.make_async_copy(coef.at[REACH], coef.at[REACH], share_send.at[i, turn]).wait()

    def handed(who, offs):
        needed, off = who
        for o in offs:

            @pl.when(inside(o) & (jnp.logical_not(needed) | (off != o)))
            def _():
                pltpu.make_async_copy(coef.at[REACH + o], coef.at[REACH + o], coef_recv.at[REACH + o]).wait()

    beside_do(halo_c, "start")
    fetch(inner_first, 0)
    beside_do(halo0, "start")
    beside_do(halo1, "start")
    def tell(i, j):
        @pl.when(t >= j)
        def _():
            pl.semaphore_signal(ready.at[i], inc=1, device_id=(t - j, s), device_id_type=MESH)

    def word(i, width):
        for ds in (width, -width):

            @pl.when(inside(ds))
            def _():
                pl.semaphore_signal(ready.at[i], inc=1, device_id=(t, s + ds), device_id_type=MESH)

    def heard(i, width):
        pl.semaphore_wait(ready.at[i], jnp.where(inside(width), 1, 0) + jnp.where(inside(-width), 1, 0))

    word(7, GREET)
    for i, j in enumerate(HOPS):
        if j <= GREET:
            tell(i, j)
    for j in range(1, FAR):

        @pl.when(seat >= j)
        def _():
            pl.semaphore_signal(ready.at[5], inc=1, device_id=(t - j, s), device_id_type=MESH)

    heard(7, GREET)
    fetch(inner_last, 0)
    for i, j in enumerate(HOPS):
        if GREET < j <= FOURTH:
            tell(i, j)

    @pl.when(group > 0)
    def _():
        word(6, FOURTH)

    @pl.when(seat < FAR - 1)
    def _():
        pl.semaphore_wait(ready.at[5], FAR - 1 - seat)

    hand_on(inner_first, 0)

    one = jnp.float32(1.0)
    own = seven(coarse[3], coarse[0], coarse[1], coarse[2], 0.5)
    beside_do(halo_c, "recv")
    stepped = inplane(own, start) + (own[1] * start_left[...] + own[2] * start_right[...])
    beside_do(halo0, "recv")
    a = pa + fine0[1] * left0[...]
    b = pb + fine1[2] * right0[...]
    pa, pb = partial(a, b)
    beside_do(halo1, "recv")
    fine_out[0] = pa + fine0[1] * (left1[1] + left1[0] * f_ref[0])
    fine_out[1] = pb + fine1[2] * (right1[1] + right1[0] * f_ref[1])
    end = restrict(work.at[0], fine_out)
    r_ref[...] = end - jnp.where(t == 0, 0.0, one) * stepped

    def each(width, slot, sem, mirrored):
        low, high = jnp.minimum(s, width), jnp.minimum(ns - 1 - s, width)
        if mirrored:
            low, high = high, low

        def one_of(i, _):
            pltpu.make_async_copy(slot(i), slot(i), sem(i)).wait()
            return 0

        lax.fori_loop(width - low, width + high + 1, one_of, 0)

    def hop(number, dt, src, slot):
        @pl.when(t + dt < nt)
        def _():
            pl.semaphore_wait(ready.at[number], 1)

            def send(ds):
                i = dt - ds
                remote(src, slot.at[i], hop_send.at[number, i], hop_recv.at[number, i], t + dt, ds).start()

            for ds in outward(dt):
                pl.when(inside(ds))(functools.partial(send, ds))
            send(0)

    def arrived(number, dt, slot):
        @pl.when(t >= dt)
        def _():
            each(dt, lambda i: slot.at[i], lambda i: hop_recv.at[number, i], False)

    def sent(number, dt, slot):
        @pl.when(t + dt < nt)
        def _():
            each(dt, lambda i: slot.at[i], lambda i: hop_send.at[number, i], True)

    for i, j in enumerate(NEAR):
        hop(i, j, r_ref, near[i])

    def factors_of(first, last):
        for i in range(first, last):
            factors = seven(coef[i, 3], coef[i, 0], coef[i, 1], coef[i, 2], 0.5)
            for n in range(7):
                kap[n, i] = factors[n]

    low, high = REACH - INNER, REACH + INNER + 1
    @pl.when(group > 0)
    def _():
        heard(6, FOURTH)
        tell(len(HOPS) - 1, FAR)

    fetch(outer, 1)
    hand_on(inner_last, 0)
    handed(inner, [o for o in range(-GREET, GREET + 1) if o])
    factors_of(low + 1, high - 1)

    def coarse_step(v):
        w = (v.shape[0] - 3) // 2
        factors = [kap[n, REACH - w : REACH + w + 1] for n in range(7)]
        return inplane(factors, v[1:-1]) + (factors[1] * v[:-2] + factors[2] * v[2:])

    for i, j in enumerate(NEAR):
        arrived(i, j, near[i])
    v = near3[...]
    v = coarse_step(v) + near2[...]
    v = coarse_step(v) + near1[...]
    u_ref[...] = coarse_step(v)[0] + r_ref[...]

    hop(3, MID, u_ref, mid)
    handed(inner, [-INNER, INNER])
    factors_of(low, low + 1)
    factors_of(high - 1, high)
    hand_on(outer, 1)
    arrived(3, MID, mid)

    @pl.when(t >= MID)
    def _():
        v = mid[...]
        for _ in range(MID):
            v = coarse_step(v)
        w_ref[...] = v[0] + u_ref[...]

    @pl.when(t < MID)
    def _():
        w_ref[...] = u_ref[...]

    hop(4, FAR, w_ref, far)

    for pair in (halo0, halo_c, halo1):
        beside_do(pair, "send")
    fetched(inner, 0)
    fetched(outer, 1)
    handed_on(inner, 0)
    handed_on(outer, 1)
    for i, j in enumerate(NEAR):
        sent(i, j, near[i])
    sent(3, MID, mid)

    @pl.when(t >= FAR)
    def _():
        handed(outer, [o for o in range(-REACH, REACH + 1) if abs(o) > INNER])
        factors_of(0, low)
        factors_of(high, 2 * REACH + 1)

    arrived(4, FAR, far)

    def finish(c):
        d = c - end
        lanes = lax.broadcasted_iota(jnp.int32, d.shape, 1)
        for h in range(2):
            wide = jnp.take_along_axis(d, lanes // 2 + 64 * h, axis=1)
            for i in range(2):
                work[0, h, pl.ds(i, d.shape[0], 2), :] = wide
            delta_out[:, 128 * h : 128 * (h + 1)] = work[0, h]

    @pl.when(t >= FAR)
    def _():
        v = far[...]
        for _ in range(FAR):
            v = coarse_step(v)
        finish(v[0] + w_ref[...])

    @pl.when(t < FAR)
    def _():
        finish(w_ref[...])

    sent(4, FAR, far)


def solution(mesh):
    nt, ns = mesh.shape["tm"], mesh.shape["space"]

    def shards(initial_states, velocity, diffusivity):
        _, planes, cy, cz = initial_states.shape
        fine = (planes, cy, cz)
        plane, small = (cy, cz), (cy // 2, cz // 2)

        def vmem(*shape):
            return pltpu.VMEM(shape, jnp.float32)

        dma = pltpu.SemaphoreType.DMA
        ended, delta = pl.pallas_call(
            lambda *refs: kernel(nt, ns, *refs),
            out_shape=(jax.ShapeDtypeStruct(fine, jnp.float32), jax.ShapeDtypeStruct(plane, jnp.float32)),
            in_specs=[pl.BlockSpec(memory_space=pltpu.HBM)] * 3,
            out_specs=(pl.BlockSpec(memory_space=pltpu.VMEM),) * 2,
            scratch_shapes=[
                vmem(*fine), vmem(3, *fine), vmem(*fine), vmem(5, 2, cy, cz // 2),
                vmem(*plane), vmem(*plane), vmem(*fine), vmem(*fine), vmem(*fine), vmem(*fine),
                vmem(*small), vmem(*small), vmem(*small),
                vmem(2 * REACH + 1, 4, *small), vmem(7, 2 * REACH + 1, *small),
                vmem(*small), vmem(*small), vmem(*small),
                *(vmem(2 * j + 1, *small) for j in NEAR), vmem(2 * MID + 1, *small), vmem(2 * FAR + 1, *small),
                dma((3,)), dma((6,)), dma((6,)), dma((2,)), dma((2 * REACH + 1,)), dma((2, FAR)),
                dma((5, 2 * FAR + 1)), dma((5, 2 * FAR + 1)),
                pltpu.SemaphoreType.REGULAR((8,)),
            ],
            compiler_params=pltpu.CompilerParams(collective_id=0, has_side_effects=True, vmem_limit_bytes=56430000),
        )(initial_states, velocity, diffusivity)
        return (ended + delta[None])[None]

    in_specs = (P("tm", "space", None, None), P(None, "space", None, None), P("space", None, None))
    out_specs = P("tm", "space", None, None)
    return jax.shard_map(shards, mesh=mesh, in_specs=in_specs, out_specs=out_specs, check_vma=False)
```
